32 devices in a mesh: blk: 8 (over z, x), rep: 4 (over y, core).
Axes of the slice: x: 2, y: 2, z: 4, core: 2. Of those that a mesh axis runs over, the one named last changes fastest.
Arguments:
- samples: bfloat16 [512, 16384], P(None, 'blk'), may hold values from -6 to 6
- theta_tiles: bfloat16 [512, 256, 256], P(('blk', 'rep')), may hold values from -6 to 6
- theta_diag: float32 [16384], P('blk'), may hold values from 0.5 to 2
- tile_row: int32 [512], P(('blk', 'rep')), may hold values from 0 to 63, as said below
- tile_col: int32 [512], P(('blk', 'rep')), may hold values from 0 to 7
- tile_count: int32 [32], P(('blk', 'rep')), may hold values from 4 to 16, as said below
Outputs:
- new_tiles: bfloat16 [512, 256, 256], P(('blk', 'rep'))
- new_diag: float32 [16384], P('blk')
The draws below stay inside these ranges and needn't reach their ends.
Inputs may be any that keep to these rules, and one draw needn't show every extreme that they name: tile_row[s] differs from the slot's block column j by 1 to 8, of either sign; pairs may repeat, and repeated tiles add. Each device's live slots are its first tile_count slots; in every blk index some device is full.
All inputs are finite; a program needn't handle non-finite values.
Results may differ from the reference program's by a relative error of at most 0.0035.
Values may be sent and summed in bfloat16 or wider, within the bound.
A program may use at most 128 MiB of HBM per device.

```python
import math
import jax
import jax.numpy as jnp
from jax import lax

B = 256
NS = 512
KB = 8
TCAP = 16
NB = 64
SLOTS = 512
DEVS = 32


def pair_draw(key):
    col_key, off_key, sign_key = jax.random.split(jax.random.fold_in(key, 11), 3)
    cols = jax.random.randint(col_key, (SLOTS,), 0, KB)
    offsets = jax.random.randint(off_key, (SLOTS,), 1, KB + 1)
    signs = jax.random.randint(sign_key, (SLOTS,), 0, 2) * 2 - 1
    group = jnp.arange(SLOTS, dtype=jnp.int32) // (SLOTS // (NB // KB))
    column = group * KB + cols
    target = column + signs * offsets
    outside = jnp.logical_or(target < 0, target >= NB)
    rows = jnp.where(outside, column - signs * offsets, target)
    return (cols.astype(jnp.int32), rows.astype(jnp.int32))


def draw_tile_col(key, part):
    return pair_draw(key)[0]


def draw_tile_row(key, part):
    return pair_draw(key)[1]


def draw_tile_count(key, part):
    key = jax.random.fold_in(key, 5)
    count_key, full_key = jax.random.split(key)
    reps = DEVS // (NB // KB)
    counts = jax.random.randint(count_key, (DEVS,), TCAP // 4, TCAP + 1)
    chosen = jax.random.randint(full_key, (DEVS // reps,), 0, reps)
    full = jnp.arange(DEVS, dtype=jnp.int32) % reps == jnp.repeat(chosen, reps, total_repeat_length=DEVS)
    return jnp.where(full, TCAP, counts).astype(jnp.int32)


def levels(own_key, shape, pieces, smallest, top_value):
    level = 1.0
    for axis_at, blocks in pieces:
        steps = jax.random.uniform(jax.random.fold_in(jax.random.fold_in(own_key, 6), axis_at), (blocks,), jnp.float32, smallest / len(pieces), top_value / len(pieces))
        level = level * jnp.repeat(jnp.exp(steps), shape[axis_at] // blocks).reshape((-1,) + (1,) * (len(shape) - 1 - axis_at))
    return level


def bell_draw(own_key, extent, scale, most, cuts=(), kind=jnp.bfloat16):
    loudness = levels(own_key, extent, cuts, -0.22, 0.18) if cuts else 1.0
    entries = jax.random.normal(own_key, extent, jnp.float32) * scale * loudness
    return jnp.minimum(jnp.maximum(entries, -most), most).astype(kind)


def setup_inputs(seed: int = 0) -> dict:
    key_list = jax.random.split(jax.random.key(seed), 7)
    samples = bell_draw(key_list[0], (NS, NB * B), 1.0, 6.0, ((1, 8),))
    theta_tiles = bell_draw(key_list[1], (SLOTS, B, B), 1.0, 6.0, ((0, 32),))
    theta_diag = jnp.clip(jnp.exp(math.log(2.0) - 1.3862944 * jax.random.uniform(key_list[2], (NB * B,), jnp.float32) ** levels(key_list[2], (NB * B,), ((0, 8),), -0.2, 0.2)), 0.5, 2.0)
    tile_row = draw_tile_row(jax.random.fold_in(key_list[6], 71), 0)
    tile_col = draw_tile_col(jax.random.fold_in(key_list[6], 71), 0)
    tile_count = draw_tile_count(jax.random.fold_in(key_list[6], 71), 0)
    return dict(samples=samples, theta_tiles=theta_tiles, theta_diag=theta_diag, tile_row=tile_row, tile_col=tile_col, tile_count=tile_count)


STEP = 0.25
PENALTY = 0.5


def reference(samples, theta_tiles, theta_diag, tile_row, tile_col, tile_count):
    groups = NB // KB
    per_group = SLOTS // groups
    slot_ids = jnp.arange(SLOTS, dtype=jnp.int32)
    live = (slot_ids % TCAP) < tile_count[slot_ids // TCAP]
    tiles = jnp.where(live[:, None, None], theta_tiles, jnp.zeros_like(theta_tiles))
    padded_x = jnp.pad(samples, ((0, 0), (KB * B, KB * B)))
    columns = jnp.arange(KB, dtype=jnp.int32)

    def group_pieces(group):
        first = (group * per_group).astype(jnp.int32)
        rows = lax.dynamic_slice_in_dim(tile_row, first, per_group) - (group - 1) * KB
        cols = lax.dynamic_slice_in_dim(tile_col, first, per_group)
        part = lax.dynamic_slice_in_dim(tiles, first, per_group, 0)
        return rows.astype(jnp.int32), cols.astype(jnp.int32), part

    def group_image(group):
        rows, cols, part = group_pieces(group)
        ext = lax.dynamic_slice_in_dim(padded_x, (group * KB * B).astype(jnp.int32), 3 * KB * B, 1)
        picked = jnp.take(ext.reshape(NS, 3 * KB, B), rows, axis=1)
        prod = jnp.einsum('sta,tab->stb', picked.astype(jnp.float32), part.astype(jnp.float32))
        onehot = (cols[:, None] == columns[None, :]).astype(jnp.float32)
        summed = jnp.einsum('stb,tk->skb', prod, onehot, precision=lax.Precision.HIGHEST)
        return summed.reshape(NS, KB * B)

    parts = lax.map(group_image, jnp.arange(groups, dtype=jnp.int32))
    image_full = jnp.transpose(parts, (1, 0, 2)).reshape(NS, NB * B)
    image_full = image_full + samples.astype(jnp.float32) * theta_diag[None, :]
    image = image_full.astype(jnp.bfloat16)
    padded_w = jnp.pad(image, ((0, 0), (KB * B, KB * B)))

    def group_update(group):
        rows, cols, part = group_pieces(group)
        start = (group * KB * B).astype(jnp.int32)
        ext_x = lax.dynamic_slice_in_dim(padded_x, start, 3 * KB * B, 1).reshape(NS, 3 * KB, B)
        ext_w = lax.dynamic_slice_in_dim(padded_w, start, 3 * KB * B, 1).reshape(NS, 3 * KB, B)
        own_x = ext_x[:, KB:2 * KB]
        own_w = ext_w[:, KB:2 * KB]
        x_row = jnp.take(ext_x, rows, axis=1).astype(jnp.float32)
        w_row = jnp.take(ext_w, rows, axis=1).astype(jnp.float32)
        x_col = jnp.take(own_x, cols, axis=1).astype(jnp.float32)
        w_col = jnp.take(own_w, cols, axis=1).astype(jnp.float32)
        first = jnp.einsum('sta,stb->tab', x_row, w_col)
        second = jnp.einsum('sta,stb->tab', w_row, x_col)
        grad = (first + second) / (2.0 * NS)
        moved = part.astype(jnp.float32) - STEP * grad
        return jnp.sign(moved) * jnp.maximum(jnp.abs(moved) - STEP * PENALTY, 0.0)

    updated = lax.map(group_update, jnp.arange(groups, dtype=jnp.int32)).reshape(SLOTS, B, B)
    new_tiles = jnp.where(live[:, None, None], updated, jnp.zeros_like(updated)).astype(jnp.bfloat16)
    dots = jnp.sum(samples.astype(jnp.float32) * image.astype(jnp.float32), axis=0) / NS
    new_diag = theta_diag - STEP * (dots - 1.0 / theta_diag)
    return new_tiles, new_diag
```

```python
import functools

import jax
import jax.numpy as jnp
from jax import lax
from jax.experimental import pallas as pl
from jax.experimental.pallas import tpu as pltpu
from jax.sharding import PartitionSpec as P

B = 256
STEP = 0.25
PENALTY = 0.5
VMEM_BYTES = 48 * 1024 * 1024
STRIP = 16


class Place:
    def __init__(self, groups):
        self.g = lax.axis_index("blk")
        self.r = lax.axis_index("rep")
        self.parity = self.g % 2
        self.core = self.r % 2
        self.half = self.r // 2
        self.partner = self.g + 1 - 2 * self.parity
        self.target = self.g + 2 - 4 * self.parity
        self.source = self.g - 2 + 4 * self.parity
        self.has_target = jnp.logical_and(self.target >= 0, self.target < groups)
        self.has_source = jnp.logical_and(self.source >= 0, self.source < groups)
        self.near = 2 * (1 - self.parity)
        self.far = 2 * self.parity

    def to_partner(self):
        return {"blk": self.partner, "rep": self.r}

    def to_target(self):
        return {"blk": self.target, "rep": self.r}

    def to_source(self):
        return {"blk": self.source, "rep": self.r}

    def to_core(self):
        return {"blk": self.g, "rep": self.r + 1 - 2 * self.core}

    def to_half(self):
        return {"blk": self.g, "rep": self.r + 2 - 4 * self.half}

    def greet(self):
        barrier = pltpu.get_barrier_semaphore()

        def signal(device):
            pl.semaphore_signal(
                barrier, inc=1, device_id=device, device_id_type=pl.DeviceIdType.MESH
            )

        signal(self.to_partner())
        signal(self.to_core())
        signal(self.to_half())

        @pl.when(self.has_target)
        def _():
            signal(self.to_target())

        @pl.when(self.has_source)
        def _():
            signal(self.to_source())

        peers = 3 + jnp.where(self.has_target, 1, 0) + jnp.where(self.has_source, 1, 0)
        pl.semaphore_wait(barrier, peers)


def remote(src, dst, send, recv, at, device):
    return pltpu.make_async_remote_copy(
        src_ref=src,
        dst_ref=dst,
        send_sem=send.at[at],
        recv_sem=recv.at[at],
        device_id=device,
        device_id_type=pl.DeviceIdType.MESH,
    )


def halo_kernel(groups, x, ext, own_sem, send, recv):
    here = Place(groups)
    unit = x.shape[0] // 8
    shared = 6 * here.half + here.core
    theirs = 6 * (1 - here.half) + here.core
    chunks = [shared, 2 + 2 * here.core, 3 + 2 * here.core]

    def rows(chunk):
        return pl.ds(pl.multiple_of(chunk * unit, unit), unit)

    def ext_at(section, chunk):
        return ext.at[section, rows(chunk), :]

    own = pltpu.make_async_copy(x, ext.at[1], own_sem)
    own.start()
    here.greet()
    near, far = here.near, here.far
    partner = [
        remote(x.at[rows(c), :], ext_at(far, c), send, recv, k, here.to_partner())
        for k, c in enumerate(chunks)
    ]
    relay = [
        remote(ext_at(near, c), ext_at(far, c), send, recv, 3 + k, here.to_target())
        for k, c in enumerate(chunks)
    ]
    across = [
        remote(ext_at(s, shared), ext_at(s, shared), send, recv, 6 + k, here.to_half())
        for k, s in enumerate([near, far])
    ]
    share_near = [
        remote(ext_at(near, c), ext_at(near, c), send, recv, 8 + k, here.to_core())
        for k, c in enumerate(chunks + [theirs])
    ]
    share_far = [
        remote(ext_at(far, c), ext_at(far, c), send, recv, 12 + k, here.to_core())
        for k, c in enumerate(chunks + [theirs])
    ]
    for copy in partner:
        copy.start()
    for k in range(3):
        partner[k].wait_recv()

        @pl.when(here.has_target)
        def _():
            relay[k].start()

        if k == 0:
            across[0].start()
        share_near[k].start()

    @pl.when(here.has_source)
    def _():
        for k in range(3):
            relay[k].wait_recv()
            if k == 0:
                across[1].start()
            share_far[k].start()

    across[0].wait_recv()
    share_near[3].start()

    @pl.when(here.has_source)
    def _():
        across[1].wait_recv()
        share_far[3].start()
        for copy in share_far:
            copy.wait_recv()
        for copy in share_far:
            copy.wait_send()
        across[1].wait_send()

    for copy in share_near:
        copy.wait_recv()
    for copy in partner + share_near + [across[0]]:
        copy.wait_send()

    @pl.when(here.has_target)
    def _():
        for copy in relay:
            copy.wait_send()

    own.wait()


def halo(x, groups):
    count, width = x.shape
    return pl.pallas_call(
        functools.partial(halo_kernel, groups),
        out_shape=jax.ShapeDtypeStruct((3, count, width), x.dtype),
        in_specs=[pl.BlockSpec(memory_space=pl.ANY)],
        out_specs=pl.BlockSpec(memory_space=pl.ANY),
        scratch_shapes=[
            pltpu.SemaphoreType.DMA,
            pltpu.SemaphoreType.DMA((16,)),
            pltpu.SemaphoreType.DMA((16,)),
        ],
        compiler_params=pltpu.CompilerParams(collective_id=0, has_side_effects=True),
        name="halo",
    )(x)


def image_kernel(slots, row, col, count, x_row, tile, out, total):
    s = pl.program_id(0)
    blocks = total.shape[0]

    @pl.when(s == 0)
    def _():
        total[...] = jnp.zeros_like(total)

    @pl.when(s < count[0])
    def _():
        total[col[s]] += jnp.dot(x_row[0], tile[0], preferred_element_type=jnp.float32)

    @pl.when(s == slots - 1)
    def _():
        for k in range(blocks):
            out[:, k * B : (k + 1) * B] = total[k].astype(out.dtype)


def partial_image(ext, tiles, row, col, count):
    _, samples, width = ext.shape
    slots = tiles.shape[0]
    blocks = width // B
    return pl.pallas_call(
        functools.partial(image_kernel, slots),
        grid_spec=pltpu.PrefetchScalarGridSpec(
            num_scalar_prefetch=3,
            grid=(slots,),
            in_specs=[
                pl.BlockSpec((1, samples, B), lambda s, row, col, n: (row[s] // blocks, 0, row[s] % blocks)),
                pl.BlockSpec((1, B, B), lambda s, row, col, n: (s, 0, 0)),
            ],
            out_specs=pl.BlockSpec((samples, width), lambda s, row, col, n: (0, 0)),
            scratch_shapes=[pltpu.VMEM((blocks, samples, B), jnp.float32)],
        ),
        out_shape=jax.ShapeDtypeStruct((samples, width), jnp.bfloat16),
        compiler_params=pltpu.CompilerParams(vmem_limit_bytes=VMEM_BYTES),
        name="partial_image",
    )(row, col, count, ext, tiles)


def reduce_kernel(groups, part, x, diag, ext, x_mine, core_in, chip_sum, half_in, final, x_sem, own_sem, send, recv):
    here = Place(groups)
    count = part.shape[0]
    quarter = count // 4
    unit = quarter // 2
    mine = 2 * here.half + here.core
    other = 2 * (1 - here.half) + here.core
    mine_core = 2 * here.half + 1 - here.core
    other_core = 2 * (1 - here.half) + 1 - here.core

    def start_row(q, k):
        return pl.multiple_of(q * quarter + k * unit, unit)

    def rows(q, k):
        return pl.ds(start_row(q, k), unit)

    def ext_at(section, q, k):
        return ext.at[section, rows(q, k), :]

    load = pltpu.make_async_copy(
        x.at[pl.ds(pl.multiple_of(mine * quarter, quarter), quarter), :], x_mine, x_sem
    )
    load.start()
    here.greet()
    near, far = here.near, here.far
    to_core = [
        remote(part.at[rows(q, k), :], core_in.at[j, k], send, recv, 2 * j + k, here.to_core())
        for j, q in enumerate([other_core, mine_core])
        for k in range(2)
    ]
    to_half = [
        remote(chip_sum.at[k], half_in.at[k], send, recv, 4 + k, here.to_half()) for k in range(2)
    ]
    gather = [
        remote(final.at[k], ext_at(1, mine, k), send, recv, 6 + k, here.to_half()) for k in range(2)
    ]
    partner = [
        remote(final.at[k], ext_at(far, mine, k), send, recv, 8 + k, here.to_partner()) for k in range(2)
    ] + [
        remote(ext_at(1, other, k), ext_at(far, other, k), send, recv, 10 + k, here.to_partner())
        for k in range(2)
    ]
    places = [(mine, 0), (mine, 1), (other, 0), (other, 1)]
    relay = [
        remote(ext_at(near, q, k), ext_at(far, q, k), send, recv, 12 + i, here.to_target())
        for i, (q, k) in enumerate(places)
    ]
    share_own = [
        remote(
            final.at[k] if i < 2 else ext_at(1, q, k), ext_at(1, q, k), send, recv, 16 + i, here.to_core()
        )
        for i, (q, k) in enumerate(places)
    ]
    share_near = [
        remote(ext_at(near, q, k), ext_at(near, q, k), send, recv, 20 + i, here.to_core())
        for i, (q, k) in enumerate(places)
    ]
    share_far = [
        remote(ext_at(far, q, k), ext_at(far, q, k), send, recv, 24 + i, here.to_core())
        for i, (q, k) in enumerate(places)
    ]
    own = [pltpu.make_async_copy(final.at[k], ext_at(1, mine, k), own_sem.at[k]) for k in range(2)]

    for copy in to_core:
        copy.start()
    for k in range(2):
        to_core[k].wait_recv()

        @pl.loop(0, unit // STRIP)
        def _(i):
            at = pl.ds(pl.multiple_of(i * STRIP, STRIP), STRIP)
            from_part = pl.ds(pl.multiple_of(start_row(other, k) + i * STRIP, STRIP), STRIP)
            both = part[from_part, :].astype(jnp.float32) + core_in[0, k, at, :].astype(jnp.float32)
            chip_sum[k, at, :] = both.astype(jnp.bfloat16)

        to_half[k].start()
    load.wait()
    for k in range(2):
        to_core[2 + k].wait_recv()
        to_half[k].wait_recv()

        @pl.loop(0, unit // STRIP)
        def _(i):
            at = pl.ds(pl.multiple_of(i * STRIP, STRIP), STRIP)
            from_part = pl.ds(pl.multiple_of(start_row(mine, k) + i * STRIP, STRIP), STRIP)
            from_x = pl.ds(pl.multiple_of(k * unit + i * STRIP, STRIP), STRIP)
            both = part[from_part, :].astype(jnp.float32) + core_in[1, k, at, :].astype(jnp.float32)
            both = both + half_in[k, at, :].astype(jnp.float32)
            final[k, at, :] = (both + x_mine[from_x, :].astype(jnp.float32) * diag[...]).astype(jnp.bfloat16)

        gather[k].start()
        partner[k].start()
        share_own[k].start()
        own[k].start()
    for k in range(2):
        gather[k].wait_recv()
        partner[2 + k].start()
        share_own[2 + k].start()
        partner[k].wait_recv()

        @pl.when(here.has_target)
        def _():
            relay[k].start()

        share_near[k].start()
    for k in range(2, 4):
        partner[k].wait_recv()

        @pl.when(here.has_target)
        def _():
            relay[k].start()

        share_near[k].start()

    @pl.when(here.has_source)
    def _():
        for k in range(4):
            relay[k].wait_recv()
            share_far[k].start()
        for copy in share_far:
            copy.wait_recv()
        for copy in share_far:
            copy.wait_send()

    for copy in share_own + share_near:
        copy.wait_recv()
    for copy in to_core + to_half + gather + partner + share_own + share_near:
        copy.wait_send()

    @pl.when(here.has_target)
    def _():
        for copy in relay:
            copy.wait_send()

    for copy in own:
        copy.wait()


def whole_image(part, x, diag, groups):
    count, width = x.shape
    quarter = count // 4
    unit = quarter // 2
    return pl.pallas_call(
        functools.partial(reduce_kernel, groups),
        out_shape=jax.ShapeDtypeStruct((3, count, width), jnp.bfloat16),
        in_specs=[
            pl.BlockSpec(memory_space=pltpu.VMEM),
            pl.BlockSpec(memory_space=pl.ANY),
            pl.BlockSpec(memory_space=pltpu.VMEM),
        ],
        out_specs=pl.BlockSpec(memory_space=pl.ANY),
        scratch_shapes=[
            pltpu.VMEM((quarter, width), jnp.bfloat16),
            pltpu.VMEM((2, 2, unit, width), jnp.bfloat16),
            pltpu.VMEM((2, unit, width), jnp.bfloat16),
            pltpu.VMEM((2, unit, width), jnp.bfloat16),
            pltpu.VMEM((2, unit, width), jnp.bfloat16),
            pltpu.SemaphoreType.DMA,
            pltpu.SemaphoreType.DMA((2,)),
            pltpu.SemaphoreType.DMA((28,)),
            pltpu.SemaphoreType.DMA((28,)),
        ],
        compiler_params=pltpu.CompilerParams(
            collective_id=1, has_side_effects=True, vmem_limit_bytes=VMEM_BYTES
        ),
        name="whole_image",
    )(part, x, diag)


def grad_kernel(scale, row, col, count, x_row, w_row, x_col, w_col, tile, out):
    s = pl.program_id(0)
    live = s < count[0]

    @pl.when(live)
    def _():
        dims = (((0,), (0,)), ((), ()))
        grad = lax.dot_general(x_row[0], w_col[0], dims, preferred_element_type=jnp.float32)
        grad += lax.dot_general(w_row[0], x_col[0], dims, preferred_element_type=jnp.float32)
        moved = tile[0].astype(jnp.float32) - (STEP * scale) * grad
        kept = jnp.maximum(jnp.abs(moved) - STEP * PENALTY, 0.0)
        out[0] = jnp.where(moved < 0, -kept, kept).astype(out.dtype)

    @pl.when(jnp.logical_not(live))
    def _():
        out[...] = jnp.zeros_like(out)


def update(ext_x, ext_w, tiles, row, col, count):
    _, samples, width = ext_x.shape
    slots = tiles.shape[0]
    blocks = width // B
    by_row = pl.BlockSpec((1, samples, B), lambda s, row, col, n: (row[s] // blocks, 0, row[s] % blocks))
    by_col = pl.BlockSpec((1, samples, B), lambda s, row, col, n: (1, 0, col[s]))
    by_slot = pl.BlockSpec((1, B, B), lambda s, row, col, n: (s, 0, 0))
    return pl.pallas_call(
        functools.partial(grad_kernel, 1.0 / (2.0 * samples)),
        grid_spec=pltpu.PrefetchScalarGridSpec(
            num_scalar_prefetch=3,
            grid=(slots,),
            in_specs=[by_row, by_row, by_col, by_col, by_slot],
            out_specs=by_slot,
        ),
        out_shape=jax.ShapeDtypeStruct(tiles.shape, jnp.bfloat16),
        compiler_params=pltpu.CompilerParams(vmem_limit_bytes=VMEM_BYTES),
        name="update",
    )(row, col, count, ext_x, ext_w, ext_x, ext_w, tiles)


def shards(samples, theta_tiles, theta_diag, tile_row, tile_col, tile_count):
    count_ns, width = samples.shape
    blocks = width // B
    groups = lax.axis_size("blk")
    group = lax.axis_index("blk")
    rows = jnp.clip(tile_row - (group - 1) * blocks, 0, 3 * blocks - 1)
    ext_x = halo(samples, groups)
    part = partial_image(ext_x, theta_tiles, rows, tile_col, tile_count)
    ext_w = whole_image(part, samples, theta_diag[None, :], groups)
    new_tiles = update(ext_x, ext_w, theta_tiles, rows, tile_col, tile_count)
    dots = jnp.sum(samples.astype(jnp.float32) * ext_w[1].astype(jnp.float32), axis=0) / count_ns
    new_diag = theta_diag - STEP * (dots - 1.0 / theta_diag)
    return (new_tiles, new_diag)


def solution(mesh):
    placed = (
        P(None, "blk"),
        P(("blk", "rep"), None, None),
        P("blk"),
        P(("blk", "rep")),
        P(("blk", "rep")),
        P(("blk", "rep")),
    )
    return jax.shard_map(
        shards,
        mesh=mesh,
        in_specs=placed,
        out_specs=(P(("blk", "rep"), None, None), P("blk")),
        check_vma=False,
    )
```

```python
import functools

import jax
import jax.numpy as jnp
from jax import lax
from jax.experimental import pallas as pl
from jax.experimental.pallas import tpu as pltpu
from jax.sharding import PartitionSpec as P

B = 256
STEP = 0.25
PENALTY = 0.5
VMEM_BYTES = 52 * 1024 * 1024


class Place:
    def __init__(self, groups):
        self.g = lax.axis_index("blk")
        self.r = lax.axis_index("rep")
        self.parity = self.g % 2
        self.core = self.r % 2
        self.half = self.r // 2
        self.partner = self.g + 1 - 2 * self.parity
        self.target = self.g + 2 - 4 * self.parity
        self.source = self.g - 2 + 4 * self.parity
        self.has_target = jnp.logical_and(self.target >= 0, self.target < groups)
        self.has_source = jnp.logical_and(self.source >= 0, self.source < groups)
        self.near = 2 * (1 - self.parity)
        self.far = 2 * self.parity

    def to_partner(self):
        return {"blk": self.partner, "rep": self.r}

    def to_target(self):
        return {"blk": self.target, "rep": self.r}

    def to_source(self):
        return {"blk": self.source, "rep": self.r}

    def to_core(self):
        return {"blk": self.g, "rep": self.r + 1 - 2 * self.core}

    def to_half(self):
        return {"blk": self.g, "rep": self.r + 2 - 4 * self.half}

    def greet(self):
        barrier = pltpu.get_barrier_semaphore()

        def signal(device):
            pl.semaphore_signal(
                barrier, inc=1, device_id=device, device_id_type=pl.DeviceIdType.MESH
            )

        signal(self.to_partner())
        signal(self.to_core())
        signal(self.to_half())

        @pl.when(self.has_target)
        def _():
            signal(self.to_target())

        @pl.when(self.has_source)
        def _():
            signal(self.to_source())

        peers = 3 + jnp.where(self.has_target, 1, 0) + jnp.where(self.has_source, 1, 0)
        pl.semaphore_wait(barrier, peers)


def remote(src, dst, send, recv, at, device):
    return pltpu.make_async_remote_copy(
        src_ref=src,
        dst_ref=dst,
        send_sem=send.at[at],
        recv_sem=recv.at[at],
        device_id=device,
        device_id_type=pl.DeviceIdType.MESH,
    )


def step_kernel(
    groups, row, prev, last, col, live, x, tiles_in, diag, out, diag_out,
    ext, img, own_img, tiles, acc, part, core_in, chip_sum, half_in, x_turned, moved, dots, dots_in,
    x_sem, tile_sem, send, recv,
):
    here = Place(groups)
    slots = tiles.shape[0]
    samples = x.shape[0]
    blocks = x.shape[1] // B
    pair = blocks // 2
    unit = samples // 8
    scale = STEP / (2.0 * samples)
    near, far = here.near, here.far

    loads = [
        pltpu.make_async_copy(x.at[:, k * B : (k + 1) * B], ext.at[blocks + k], x_sem.at[k])
        for k in range(blocks)
    ]
    for load in loads:
        load.start()
    tile_load = pltpu.make_async_copy(tiles_in, tiles, tile_sem)
    tile_load.start()
    acc[0] = jnp.zeros_like(acc[0])
    here.greet()

    shared = 6 * here.half + here.core
    theirs = 6 * (1 - here.half) + here.core
    chunks = [shared, 2 + 2 * here.core, 3 + 2 * here.core]

    def x_at(section, chunk):
        return ext.at[pl.ds(section * blocks, blocks), pl.ds(pl.multiple_of(chunk * unit, unit), unit), :]

    partner = [
        remote(x_at(1, c), x_at(far, c), send, recv, k, here.to_partner()) for k, c in enumerate(chunks)
    ]
    relay = [
        remote(x_at(near, c), x_at(far, c), send, recv, 3 + k, here.to_target())
        for k, c in enumerate(chunks)
    ]
    across = [
        remote(x_at(s, shared), x_at(s, shared), send, recv, 6 + k, here.to_half())
        for k, s in enumerate([near, far])
    ]
    share_near = [
        remote(x_at(near, c), x_at(near, c), send, recv, 8 + k, here.to_core())
        for k, c in enumerate(chunks + [theirs])
    ]
    share_far = [
        remote(x_at(far, c), x_at(far, c), send, recv, 12 + k, here.to_core())
        for k, c in enumerate(chunks + [theirs])
    ]
    for load in loads:
        load.wait()
    for copy in partner:
        copy.start()
    for k in range(3):
        partner[k].wait_recv()

        @pl.when(here.has_target)
        def _():
            relay[k].start()

        if k == 0:
            across[0].start()
        share_near[k].start()

    @pl.when(here.has_source)
    def _():
        for k in range(3):
            relay[k].wait_recv()
            if k == 0:
                across[1].start()
            share_far[k].start()

    across[0].wait_recv()
    share_near[3].start()

    @pl.when(here.has_source)
    def _():
        across[1].wait_recv()
        share_far[3].start()
        for copy in share_far:
            copy.wait_recv()
        for copy in share_far:
            copy.wait_send()
        across[1].wait_send()

    for copy in share_near:
        copy.wait_recv()
    for copy in partner + share_near + [across[0]]:
        copy.wait_send()

    @pl.when(here.has_target)
    def _():
        for copy in relay:
            copy.wait_send()

    tile_load.wait()

    @pl.loop(0, slots)
    def _(s):
        acc[s + 1] = acc[prev[s]] + jnp.dot(ext[row[s]], tiles[s], preferred_element_type=jnp.float32)

    quarter = samples // 4
    mine = 2 * here.half + here.core
    other = 2 * (1 - here.half) + here.core
    mine_core = 2 * here.half + 1 - here.core
    other_core = 2 * (1 - here.half) + 1 - here.core

    def rows(q):
        return pl.ds(pl.multiple_of(q * quarter, quarter), quarter)

    def part_at(q, h):
        return part.at[pl.ds(h * pair, pair), rows(q), :]

    def img_at(section, q, h):
        return img.at[pl.ds(section * blocks + h * pair, pair), q]

    def own_at(q, h):
        return own_img.at[pl.ds(h * pair, pair), q]

    to_core = [
        remote(part_at(q, h), core_in.at[j, h], send, recv, 16 + 2 * j + h, here.to_core())
        for j, q in enumerate([other_core, mine_core])
        for h in range(2)
    ]
    to_half = [
        remote(chip_sum.at[h], half_in.at[h], send, recv, 20 + h, here.to_half()) for h in range(2)
    ]
    gather = [
        remote(own_at(mine, h), own_at(mine, h), send, recv, 22 + h, here.to_half())
        for h in range(2)
    ]
    places = [(mine, 0), (mine, 1), (other, 0), (other, 1)]
    partner_w = [
        remote(own_at(q, h), img_at(far, q, h), send, recv, 24 + i, here.to_partner())
        for i, (q, h) in enumerate(places)
    ]
    relay_w = [
        remote(img_at(near, q, h), img_at(far, q, h), send, recv, 28 + i, here.to_target())
        for i, (q, h) in enumerate(places)
    ]
    share_own_w = [
        remote(own_at(q, h), own_at(q, h), send, recv, 32 + i, here.to_core())
        for i, (q, h) in enumerate(places)
    ]
    share_near_w, share_far_w = [
        [
            remote(img_at(s, q, h), img_at(s, q, h), send, recv, first + i, here.to_core())
            for i, (q, h) in enumerate(places)
        ]
        for s, first in [(near, 36), (far, 40)]
    ]
    dots_core = remote(dots.at[0], dots_in.at[0], send, recv, 44, here.to_core())
    dots_half = remote(dots.at[1], dots_in.at[1], send, recv, 45, here.to_half())

    for h in range(2):

        @pl.loop(h * pair, (h + 1) * pair)
        def _(k):
            part[k] = acc[last[k]].astype(jnp.bfloat16)

        to_core[h].start()
        to_core[2 + h].start()
    for h in range(2):
        to_core[h].wait_recv()

        @pl.loop(0, pair)
        def _(j):
            both = part[h * pair + j, rows(other), :].astype(jnp.float32) + core_in[0, h, j].astype(jnp.float32)
            chip_sum[h, j] = both.astype(jnp.bfloat16)

        to_half[h].start()

    @pl.loop(0, slots)
    def _(s):
        x_turned[s] = ext[row[s]].T

    for h in range(2):
        to_core[2 + h].wait_recv()
        to_half[h].wait_recv()
        for j in range(pair):
            k = h * pair + j
            lanes = pl.ds(k * B, B)
            xs = ext[blocks + k, rows(mine), :].astype(jnp.float32)
            both = part[k, rows(mine), :].astype(jnp.float32) + core_in[1, h, j].astype(jnp.float32)
            both = both + half_in[h, j].astype(jnp.float32) + xs * diag[:, lanes]
            rounded = both.astype(jnp.bfloat16)
            own_img[k, mine] = rounded.T
            dots[0, k : k + 1, :] = jnp.sum(xs * rounded.astype(jnp.float32), axis=0, keepdims=True)
        gather[h].start()
        partner_w[h].start()
        share_own_w[h].start()
    dots_core.start()
    for h in range(2):
        gather[h].wait_recv()
        partner_w[2 + h].start()
        share_own_w[2 + h].start()
        partner_w[h].wait_recv()

        @pl.when(here.has_target)
        def _():
            relay_w[h].start()

        share_near_w[h].start()
    dots_core.wait_recv()
    dots[1] = dots[0] + dots_in[0]
    dots_half.start()
    for copy in share_own_w:
        copy.wait_recv()

    def turned(ref, at):
        return jnp.concatenate([ref[at, q] for q in range(4)], axis=1)

    def first_half(start, end):
        @pl.loop(start, end)
        def _(s):
            grad = lax.dot_general(
                x_turned[s], turned(own_img, col[s]), (((1,), (1,)), ((), ())),
                preferred_element_type=jnp.float32,
            )
            moved[s] = tiles[s].astype(jnp.float32) - scale * grad

    first_half(0, slots // 2)

    @pl.loop(0, blocks)
    def _(k):
        img[blocks + k] = own_img[k]

    partner_w[2].wait_recv()

    @pl.when(here.has_target)
    def _():
        relay_w[2].start()

    share_near_w[2].start()
    first_half(slots // 2, slots)
    partner_w[3].wait_recv()

    @pl.when(here.has_target)
    def _():
        relay_w[3].start()

    share_near_w[3].start()
    dots_half.wait_recv()
    for k in range(blocks):
        lanes = pl.ds(k * B, B)
        total = dots[1, k : k + 1, :] + dots_in[1, k : k + 1, :]
        old = diag[:, lanes]
        diag_out[:, lanes] = old - STEP * (total / samples - 1.0 / old)

    @pl.when(here.has_source)
    def _():
        for i in range(4):
            relay_w[i].wait_recv()
            share_far_w[i].start()
        for copy in share_far_w:
            copy.wait_recv()

    for copy in share_near_w:
        copy.wait_recv()

    @pl.loop(0, slots)
    def _(s):
        grad = jnp.dot(turned(img, row[s]), ext[blocks + col[s]], preferred_element_type=jnp.float32)
        value = moved[s] - scale * grad
        kept = jnp.maximum(jnp.abs(value) - STEP * PENALTY, 0.0)
        signed = jnp.where(value < 0, -kept, kept)
        out[s] = jnp.where(s < live[0], signed, 0.0).astype(out.dtype)

    for copy in to_core + to_half + gather + partner_w + share_own_w + share_near_w + [dots_core, dots_half]:
        copy.wait_send()

    @pl.when(here.has_target)
    def _():
        for copy in relay_w:
            copy.wait_send()

    @pl.when(here.has_source)
    def _():
        for copy in share_far_w:
            copy.wait_send()


def step(x, tiles, diag, row, prev, last, col, live, groups):
    samples, width = x.shape
    slots = tiles.shape[0]
    blocks = width // B
    pair = blocks // 2
    quarter = samples // 4
    bf16, f32 = jnp.bfloat16, jnp.float32
    smem = pl.BlockSpec(memory_space=pltpu.SMEM)
    vmem = pl.BlockSpec(memory_space=pltpu.VMEM)
    hbm = pl.BlockSpec(memory_space=pl.ANY)
    return pl.pallas_call(
        functools.partial(step_kernel, groups),
        out_shape=(
            jax.ShapeDtypeStruct(tiles.shape, bf16),
            jax.ShapeDtypeStruct(diag.shape, f32),
        ),
        in_specs=[smem, smem, smem, smem, smem, hbm, hbm, vmem],
        out_specs=(vmem, vmem),
        scratch_shapes=[
            pltpu.VMEM((3 * blocks, samples, B), bf16),
            pltpu.VMEM((3 * blocks, 4, B, quarter), bf16),
            pltpu.VMEM((blocks, 4, B, quarter), bf16),
            pltpu.VMEM(tiles.shape, bf16),
            pltpu.VMEM((slots + 1, samples, B), f32),
            pltpu.VMEM((blocks, samples, B), bf16),
            pltpu.VMEM((2, 2, pair, quarter, B), bf16),
            pltpu.VMEM((2, pair, quarter, B), bf16),
            pltpu.VMEM((2, pair, quarter, B), bf16),
            pltpu.VMEM((slots, B, samples), bf16),
            pltpu.VMEM((slots, B, B), f32),
            pltpu.VMEM((2, blocks, B), f32),
            pltpu.VMEM((2, blocks, B), f32),
            pltpu.SemaphoreType.DMA((blocks,)),
            pltpu.SemaphoreType.DMA,
            pltpu.SemaphoreType.DMA((46,)),
            pltpu.SemaphoreType.DMA((46,)),
        ],
        compiler_params=pltpu.CompilerParams(
            collective_id=0, has_side_effects=True, vmem_limit_bytes=VMEM_BYTES
        ),
        name="step",
    )(row, prev, last, col, live, x, tiles, diag)


def shards(samples, theta_tiles, theta_diag, tile_row, tile_col, tile_count):
    blocks = samples.shape[1] // B
    slots = theta_tiles.shape[0]
    groups = lax.axis_size("blk")
    group = lax.axis_index("blk")
    rows = jnp.clip(tile_row - (group - 1) * blocks, 0, 3 * blocks - 1)
    at = jnp.arange(slots, dtype=jnp.int32)
    linked = jnp.where(at < tile_count[0], at + 1, 0)
    same = jnp.logical_and(tile_col[:, None] == tile_col[None, :], at[None, :] < at[:, None])
    prev = jnp.max(jnp.where(same, linked[None, :], 0), axis=1)
    hit = tile_col[None, :] == jnp.arange(blocks, dtype=jnp.int32)[:, None]
    last = jnp.max(jnp.where(hit, linked[None, :], 0), axis=1)
    new_tiles, new_diag = step(
        samples, theta_tiles, theta_diag[None, :], rows, prev, last, tile_col, tile_count, groups
    )
    return (new_tiles, new_diag[0])


def solution(mesh):
    placed = (
        P(None, "blk"),
        P(("blk", "rep"), None, None),
        P("blk"),
        P(("blk", "rep")),
        P(("blk", "rep")),
        P(("blk", "rep")),
    )
    return jax.shard_map(
        shards,
        mesh=mesh,
        in_specs=placed,
        out_specs=(P(("blk", "rep"), None, None), P("blk")),
        check_vma=False,
    )
```

```python
import functools

import jax
import jax.numpy as jnp
from jax import lax
from jax.experimental import pallas as pl
from jax.experimental.pallas import tpu as pltpu
from jax.sharding import PartitionSpec as P

B = 256
STEP = 0.25
PENALTY = 0.5
VMEM_BYTES = 40 * 1024 * 1024


class Place:
    def __init__(self, groups):
        self.g = lax.axis_index("blk")
        self.r = lax.axis_index("rep")
        self.parity = self.g % 2
        self.core = self.r % 2
        self.half = self.r // 2
        self.partner = self.g + 1 - 2 * self.parity
        self.target = self.g + 2 - 4 * self.parity
        self.source = self.g - 2 + 4 * self.parity
        self.has_target = jnp.logical_and(self.target >= 0, self.target < groups)
        self.has_source = jnp.logical_and(self.source >= 0, self.source < groups)
        self.near = 2 * (1 - self.parity)
        self.far = 2 * self.parity

    def to_partner(self):
        return {"blk": self.partner, "rep": self.r}

    def to_target(self):
        return {"blk": self.target, "rep": self.r}

    def to_source(self):
        return {"blk": self.source, "rep": self.r}

    def to_core(self):
        return {"blk": self.g, "rep": self.r + 1 - 2 * self.core}

    def to_half(self):
        return {"blk": self.g, "rep": self.r + 2 - 4 * self.half}

    def greet(self):
        barrier = pltpu.get_barrier_semaphore()

        def signal(device):
            pl.semaphore_signal(
                barrier, inc=1, device_id=device, device_id_type=pl.DeviceIdType.MESH
            )

        signal(self.to_partner())
        signal(self.to_core())
        signal(self.to_half())

        @pl.when(self.has_target)
        def _():
            signal(self.to_target())

        @pl.when(self.has_source)
        def _():
            signal(self.to_source())

        peers = 3 + jnp.where(self.has_target, 1, 0) + jnp.where(self.has_source, 1, 0)
        pl.semaphore_wait(barrier, peers)


def remote(src, dst, send, recv, at, device):
    return pltpu.make_async_remote_copy(
        src_ref=src,
        dst_ref=dst,
        send_sem=send.at[at],
        recv_sem=recv.at[at],
        device_id=device,
        device_id_type=pl.DeviceIdType.MESH,
    )


HALVES = 2
COPIES = 42


class Half:
    def __init__(self, here, first, ext, img, own_img, part, core_in, chip_sum, half_in, send, recv):
        self.here = here
        self.ext, self.img, self.own_img = ext, img, own_img
        self.part, self.core_in, self.chip_sum, self.half_in = part, core_in, chip_sum, half_in
        blocks, samples, _ = part.shape
        unit = samples // 8
        near, far = here.near, here.far
        self.mine = 2 * here.half + here.core
        self.other = 2 * (1 - here.half) + here.core
        self.mine_core = 2 * here.half + 1 - here.core
        self.other_core = 2 * (1 - here.half) + 1 - here.core
        self.owned = blocks // 4
        owned = self.owned

        def copy(src, dst, at, device):
            return remote(src, dst, send, recv, first + at, device)

        shared = 6 * here.half + here.core
        theirs = 6 * (1 - here.half) + here.core
        chunks = [shared, 2 + 2 * here.core, 3 + 2 * here.core]

        def x_at(section, chunk):
            rows = pl.ds(pl.multiple_of(chunk * unit, unit), unit)
            return ext.at[pl.ds(section * blocks, blocks), rows, :]

        self.partner = [
            copy(x_at(1, c), x_at(far, c), k, here.to_partner()) for k, c in enumerate(chunks)
        ]
        self.relay = [
            copy(x_at(near, c), x_at(far, c), 3 + k, here.to_target()) for k, c in enumerate(chunks)
        ]
        self.across = [
            copy(x_at(s, shared), x_at(s, shared), 6 + k, here.to_half()) for k, s in enumerate([near, far])
        ]
        self.share_near, self.share_far = [
            [copy(x_at(s, c), x_at(s, c), at + k, here.to_core()) for k, c in enumerate(chunks + [theirs])]
            for s, at in [(near, 8), (far, 12)]
        ]

        def img_at(section, q, e):
            return img.at[section * blocks + q * owned + e]

        def own_at(q, e):
            return own_img.at[q * owned + e]

        self.to_core = [
            copy(part.at[pl.ds(q * owned, owned)], core_in.at[j], 16 + j, here.to_core())
            for j, q in enumerate([self.other_core, self.mine_core])
        ]
        self.to_half = [copy(chip_sum.at[e], half_in.at[e], 18 + e, here.to_half()) for e in range(2)]
        self.gather = [
            copy(own_at(self.mine, e), own_at(self.mine, e), 20 + e, here.to_half()) for e in range(2)
        ]
        places = [(self.mine, 0), (self.mine, 1), (self.other, 0), (self.other, 1)]
        self.partner_w = [
            copy(own_at(q, e), img_at(far, q, e), 22 + i, here.to_partner())
            for i, (q, e) in enumerate(places)
        ]
        self.relay_w = [
            copy(img_at(near, q, e), img_at(far, q, e), 26 + i, here.to_target())
            for i, (q, e) in enumerate(places)
        ]
        self.share_own_w = [
            copy(own_at(q, e), own_at(q, e), 30 + i, here.to_core()) for i, (q, e) in enumerate(places)
        ]
        self.share_near_w, self.share_far_w = [
            [
                copy(img_at(s, q, e), img_at(s, q, e), at + i, here.to_core())
                for i, (q, e) in enumerate(places)
            ]
            for s, at in [(near, 34), (far, 38)]
        ]

    def send_x(self):
        for copy in self.partner:
            copy.start()

    def pass_x(self, k):
        self.partner[k].wait_recv()

        @pl.when(self.here.has_target)
        def _():
            self.relay[k].start()

        if k == 0:
            self.across[0].start()
        self.share_near[k].start()

    def end_x(self):
        @pl.when(self.here.has_source)
        def _():
            for k in range(3):
                self.relay[k].wait_recv()
                if k == 0:
                    self.across[1].start()
                self.share_far[k].start()

        self.across[0].wait_recv()
        self.share_near[3].start()

        @pl.when(self.here.has_source)
        def _():
            self.across[1].wait_recv()
            self.share_far[3].start()
            for copy in self.share_far:
                copy.wait_recv()

        for copy in self.share_near:
            copy.wait_recv()

    def sum_slots(self, acc, row, prev, last, tiles):
        @pl.loop(0, tiles.shape[0])
        def _(s):
            product = jnp.dot(self.ext[row[s]], tiles[s], preferred_element_type=jnp.float32)
            acc[s + 1] = acc[prev[s]] + product

        for j, q in enumerate([self.other_core, self.mine_core, self.other, self.mine]):
            for e in range(2):
                k = q * self.owned + e
                self.part[k] = acc[last[k]].astype(jnp.bfloat16)
            if j < 2:
                self.to_core[j].start()

    def sum_chip(self):
        self.to_core[0].wait_recv()
        for e in range(2):
            both = self.part[self.other * self.owned + e].astype(jnp.float32)
            both = both + self.core_in[0, e].astype(jnp.float32)
            self.chip_sum[e] = both.astype(jnp.bfloat16)
            self.to_half[e].start()

    def finish_image(self, diag, dots):
        self.to_core[1].wait_recv()
        blocks = self.part.shape[0]
        for e in range(2):
            self.to_half[e].wait_recv()
            k = self.mine * self.owned + e
            xs = self.ext[blocks + k].astype(jnp.float32)
            both = self.part[k].astype(jnp.float32) + self.core_in[1, e].astype(jnp.float32)
            both = both + self.half_in[e].astype(jnp.float32) + xs * diag[pl.ds(k, 1), :]
            rounded = both.astype(jnp.bfloat16)
            self.own_img[k] = rounded.T
            self.partner_w[e].start()
            self.gather[e].start()
            self.share_own_w[e].start()
            dots[0, pl.ds(k, 1), :] += jnp.sum(xs * rounded.astype(jnp.float32), axis=0, keepdims=True)

    def pass_gathered(self, e):
        self.gather[e].wait_recv()
        self.partner_w[2 + e].start()
        self.share_own_w[2 + e].start()

    def pass_w(self, i):
        self.partner_w[i].wait_recv()

        @pl.when(self.here.has_target)
        def _():
            self.relay_w[i].start()

        self.share_near_w[i].start()

    def end_own_w(self):
        for copy in self.share_own_w:
            copy.wait_recv()
        blocks = self.part.shape[0]

        @pl.loop(0, blocks)
        def _(k):
            self.img[blocks + k] = self.own_img[k]

    def end_w(self):
        @pl.when(self.here.has_source)
        def _():
            for i in range(4):
                self.relay_w[i].wait_recv()
                self.share_far_w[i].start()
            for copy in self.share_far_w:
                copy.wait_recv()

        for copy in self.share_near_w:
            copy.wait_recv()

    def drain(self):
        for copies in [
            self.partner, self.share_near, self.across[:1], self.to_core, self.to_half, self.gather,
            self.partner_w, self.share_own_w, self.share_near_w,
        ]:
            for copy in copies:
                copy.wait_send()

        @pl.when(self.here.has_target)
        def _():
            for copy in self.relay + self.relay_w:
                copy.wait_send()

        @pl.when(self.here.has_source)
        def _():
            for copy in self.share_far + self.across[1:] + self.share_far_w:
                copy.wait_send()


def step_kernel(
    groups, row_in, col, live, x, tiles_in, diag_in, out, diag_out,
    ext_a, ext_b, img_a, img_b, own_a, own_b, part_a, part_b, core_a, core_b, chip_a, chip_b, half_a, half_b,
    tiles, acc, x_turned, moved, diag_flat, diag, dots, dots_in, row, prev, last,
    x_sem, tile_sem, diag_sem, send, recv,
):
    here = Place(groups)
    slots = tiles.shape[0]
    samples = x.shape[0]
    blocks = x.shape[1] // B
    cut = samples // HALVES
    scale = STEP / (2.0 * samples)
    a = Half(here, 0, ext_a, img_a, own_a, part_a, core_a, chip_a, half_a, send, recv)
    b = Half(here, COPIES, ext_b, img_b, own_b, part_b, core_b, chip_b, half_b, send, recv)
    dots_core = remote(dots.at[0], dots_in.at[0], send, recv, 2 * COPIES, here.to_core())
    dots_half = remote(dots.at[1], dots_in.at[1], send, recv, 2 * COPIES + 1, here.to_half())

    loads = [
        [
            pltpu.make_async_copy(
                x.at[h * cut : (h + 1) * cut, k * B : (k + 1) * B], half.ext.at[blocks + k], x_sem.at[h, k]
            )
            for k in range(blocks)
        ]
        for h, half in enumerate([a, b])
    ]
    for load in loads[0] + loads[1]:
        load.start()
    diag_load = pltpu.make_async_copy(diag_in, diag_flat, diag_sem)
    diag_load.start()
    tile_load = pltpu.make_async_copy(tiles_in, tiles, tile_sem)
    tile_load.start()
    here.greet()
    for load in loads[0]:
        load.wait()
    a.send_x()

    def latest(column, end):
        def later(t, best):
            return jnp.where(jnp.logical_and(t < live[0], col[t] == column), t + 1, best)

        return lax.fori_loop(0, end, later, jnp.int32(0))

    @pl.loop(0, slots)
    def _(s):
        row[s] = jnp.clip(row_in[s] - (here.g - 1) * blocks, 0, 3 * blocks - 1)
        prev[s] = latest(col[s], s)

    @pl.loop(0, blocks)
    def _(k):
        last[k] = latest(k, slots)

    acc[0] = jnp.zeros_like(acc[0])
    dots[0] = jnp.zeros_like(dots[0])
    diag_load.wait()
    for k in range(blocks):
        diag[k : k + 1, :] = diag_flat[:, k * B : (k + 1) * B]
    for load in loads[1]:
        load.wait()
    tile_load.wait()

    def turn(half, at):
        @pl.loop(0, slots)
        def _(s):
            x_turned[at, s] = half.ext[row[s]].T

    def own_grad(half, at, s):
        return lax.dot_general(
            x_turned[at, s], half.own_img[col[s]], (((1,), (1,)), ((), ())),
            preferred_element_type=jnp.float32,
        )

    def row_grad(half, s):
        return jnp.dot(half.img[row[s]], half.ext[blocks + col[s]], preferred_element_type=jnp.float32)

    for k in range(3):
        a.pass_x(k)
    b.send_x()
    a.end_x()
    b.pass_x(0)
    a.sum_slots(acc, row, prev, last, tiles)
    b.pass_x(1)
    a.sum_chip()
    b.pass_x(2)
    turn(a, 0)
    b.end_x()
    b.sum_slots(acc, row, prev, last, tiles)
    a.finish_image(diag, dots)
    b.sum_chip()
    for e in range(2):
        a.pass_gathered(e)
        a.pass_w(e)
    turn(b, 1)
    b.finish_image(diag, dots)
    dots_core.start()
    a.pass_w(2)
    a.pass_w(3)
    for e in range(2):
        b.pass_gathered(e)
        b.pass_w(e)
    dots_core.wait_recv()
    dots[1] = dots[0] + dots_in[0]
    dots_half.start()
    a.end_own_w()
    a.end_w()

    def first_half(start, end):
        @pl.loop(start, end)
        def _(s):
            moved[s] = tiles[s].astype(jnp.float32) - scale * (own_grad(a, 0, s) + row_grad(a, s))

    first_half(0, slots // 2)
    b.pass_w(2)
    first_half(slots // 2, slots)
    b.pass_w(3)
    b.end_own_w()

    @pl.loop(0, slots)
    def _(s):
        moved[s] -= scale * own_grad(b, 1, s)

    dots_half.wait_recv()
    for k in range(blocks):
        total = dots[1, k : k + 1, :] + dots_in[1, k : k + 1, :]
        old = diag[k : k + 1, :]
        diag_out[:, k * B : (k + 1) * B] = old - STEP * (total / samples - 1.0 / old)
    b.end_w()

    @pl.loop(0, slots)
    def _(s):
        value = moved[s] - scale * row_grad(b, s)
        kept = jnp.maximum(jnp.abs(value) - STEP * PENALTY, 0.0)
        signed = jnp.where(value < 0, -kept, kept)
        out[s] = jnp.where(s < live[0], signed, 0.0).astype(out.dtype)

    a.drain()
    b.drain()
    dots_core.wait_send()
    dots_half.wait_send()


def step(x, tiles, diag, row, col, live, groups):
    samples, width = x.shape
    slots = tiles.shape[0]
    blocks = width // B
    owned = blocks // 4
    cut = samples // HALVES
    bf16, f32 = jnp.bfloat16, jnp.float32
    smem = pl.BlockSpec(memory_space=pltpu.SMEM)
    vmem = pl.BlockSpec(memory_space=pltpu.VMEM)
    hbm = pl.BlockSpec(memory_space=pl.ANY)

    def twice(*shape):
        return [pltpu.VMEM(shape, bf16)] * 2

    return pl.pallas_call(
        functools.partial(step_kernel, groups),
        out_shape=(
            jax.ShapeDtypeStruct(tiles.shape, bf16),
            jax.ShapeDtypeStruct(diag.shape, f32),
        ),
        in_specs=[smem, smem, smem, hbm, hbm, hbm],
        out_specs=(vmem, vmem),
        scratch_shapes=twice(3 * blocks, cut, B)
        + twice(3 * blocks, B, cut)
        + twice(blocks, B, cut)
        + twice(blocks, cut, B)
        + twice(2, owned, cut, B)
        + twice(owned, cut, B)
        + twice(owned, cut, B)
        + [
            pltpu.VMEM(tiles.shape, bf16),
            pltpu.VMEM((slots + 1, cut, B), f32),
            pltpu.VMEM((2, slots, B, cut), bf16),
            pltpu.VMEM((slots, B, B), f32),
            pltpu.VMEM(diag.shape, f32),
            pltpu.VMEM((blocks, B), f32),
            pltpu.VMEM((2, blocks, B), f32),
            pltpu.VMEM((2, blocks, B), f32),
            pltpu.SMEM((slots,), jnp.int32),
            pltpu.SMEM((slots,), jnp.int32),
            pltpu.SMEM((blocks,), jnp.int32),
            pltpu.SemaphoreType.DMA((2, blocks)),
            pltpu.SemaphoreType.DMA,
            pltpu.SemaphoreType.DMA,
            pltpu.SemaphoreType.DMA((2 * COPIES + 2,)),
            pltpu.SemaphoreType.DMA((2 * COPIES + 2,)),
        ],
        compiler_params=pltpu.CompilerParams(
            collective_id=0, has_side_effects=True, vmem_limit_bytes=VMEM_BYTES
        ),
        name="step",
    )(row, col, live, x, tiles, diag)


def shards(samples, theta_tiles, theta_diag, tile_row, tile_col, tile_count):
    groups = lax.axis_size("blk")
    new_tiles, new_diag = step(
        samples, theta_tiles, theta_diag[None, :], tile_row, tile_col, tile_count, groups
    )
    return (new_tiles, new_diag[0])


def solution(mesh):
    placed = (
        P(None, "blk"),
        P(("blk", "rep"), None, None),
        P("blk"),
        P(("blk", "rep")),
        P(("blk", "rep")),
        P(("blk", "rep")),
    )
    return jax.shard_map(
        shards,
        mesh=mesh,
        in_specs=placed,
        out_specs=(P(("blk", "rep"), None, None), P("blk")),
        check_vma=False,
    )
```

```python
import functools

import jax
import jax.numpy as jnp
from jax import lax
from jax.experimental import pallas as pl
from jax.experimental.pallas import tpu as pltpu
from jax.sharding import PartitionSpec as P

B = 256
STEP = 0.25
PENALTY = 0.5
VMEM_BYTES = 50 * 1024 * 1024


class Place:
    def __init__(self, groups):
        self.g = lax.axis_index("blk")
        self.r = lax.axis_index("rep")
        self.parity = self.g % 2
        self.core = self.r % 2
        self.half = self.r // 2
        self.partner = self.g + 1 - 2 * self.parity
        self.target = self.g + 2 - 4 * self.parity
        self.source = self.g - 2 + 4 * self.parity
        self.has_target = jnp.logical_and(self.target >= 0, self.target < groups)
        self.has_source = jnp.logical_and(self.source >= 0, self.source < groups)
        self.near = 2 * (1 - self.parity)
        self.far = 2 * self.parity

    def to_partner(self):
        return {"blk": self.partner, "rep": self.r}

    def to_target(self):
        return {"blk": self.target, "rep": self.r}

    def to_source(self):
        return {"blk": self.source, "rep": self.r}

    def to_core(self):
        return {"blk": self.g, "rep": self.r + 1 - 2 * self.core}

    def to_half(self):
        return {"blk": self.g, "rep": self.r + 2 - 4 * self.half}

    def greet(self):
        barrier = pltpu.get_barrier_semaphore()

        def signal(device):
            pl.semaphore_signal(
                barrier, inc=1, device_id=device, device_id_type=pl.DeviceIdType.MESH
            )

        signal(self.to_partner())
        signal(self.to_core())
        signal(self.to_half())

        @pl.when(self.has_target)
        def _():
            signal(self.to_target())

        @pl.when(self.has_source)
        def _():
            signal(self.to_source())

        peers = 3 + jnp.where(self.has_target, 1, 0) + jnp.where(self.has_source, 1, 0)
        pl.semaphore_wait(barrier, peers)


def remote(src, dst, send, recv, at, device):
    return pltpu.make_async_remote_copy(
        src_ref=src,
        dst_ref=dst,
        send_sem=send.at[at],
        recv_sem=recv.at[at],
        device_id=device,
        device_id_type=pl.DeviceIdType.MESH,
    )


HALVES = 2
UNROLL = 4
COPIES = 42


class Half:
    def __init__(self, here, first, ext, img, own_img, part, core_in, chip_sum, half_in, send, recv):
        self.here = here
        self.ext, self.img, self.own_img = ext, img, own_img
        self.part, self.core_in, self.chip_sum, self.half_in = part, core_in, chip_sum, half_in
        blocks, samples, _ = part.shape
        unit = samples // 8
        near, far = here.near, here.far
        self.mine = 2 * here.half + here.core
        self.other = 2 * (1 - here.half) + here.core
        self.mine_core = 2 * here.half + 1 - here.core
        self.other_core = 2 * (1 - here.half) + 1 - here.core
        self.owned = blocks // 4
        owned = self.owned

        def copy(src, dst, at, device):
            return remote(src, dst, send, recv, first + at, device)

        shared = 6 * here.half + here.core
        theirs = 6 * (1 - here.half) + here.core
        chunks = [shared, 2 + 2 * here.core, 3 + 2 * here.core]

        def x_at(section, chunk):
            rows = pl.ds(pl.multiple_of(chunk * unit, unit), unit)
            return ext.at[pl.ds(section * blocks, blocks), rows, :]

        self.partner = [
            copy(x_at(1, c), x_at(far, c), k, here.to_partner()) for k, c in enumerate(chunks)
        ]
        self.relay = [
            copy(x_at(near, c), x_at(far, c), 3 + k, here.to_target()) for k, c in enumerate(chunks)
        ]
        self.across = [
            copy(x_at(s, shared), x_at(s, shared), 6 + k, here.to_half()) for k, s in enumerate([near, far])
        ]
        self.share_near, self.share_far = [
            [copy(x_at(s, c), x_at(s, c), at + k, here.to_core()) for k, c in enumerate(chunks + [theirs])]
            for s, at in [(near, 8), (far, 12)]
        ]

        def img_at(section, q, e):
            return img.at[section * blocks + q * owned + e]

        def own_at(q, e):
            return own_img.at[q * owned + e]

        self.to_core = [
            copy(part.at[pl.ds(q * owned, owned)], core_in.at[j], 16 + j, here.to_core())
            for j, q in enumerate([self.other_core, self.mine_core])
        ]
        self.to_half = [copy(chip_sum.at[e], half_in.at[e], 18 + e, here.to_half()) for e in range(2)]
        self.gather = [
            copy(own_at(self.mine, e), own_at(self.mine, e), 20 + e, here.to_half()) for e in range(2)
        ]
        places = [(self.mine, 0), (self.mine, 1), (self.other, 0), (self.other, 1)]
        self.partner_w = [
            copy(own_at(q, e), img_at(far, q, e), 22 + i, here.to_partner())
            for i, (q, e) in enumerate(places)
        ]
        self.relay_w = [
            copy(img_at(near, q, e), img_at(far, q, e), 26 + i, here.to_target())
            for i, (q, e) in enumerate(places)
        ]
        self.share_own_w = [
            copy(own_at(q, e), own_at(q, e), 30 + i, here.to_core()) for i, (q, e) in enumerate(places)
        ]
        self.share_near_w, self.share_far_w = [
            [
                copy(img_at(s, q, e), img_at(s, q, e), at + i, here.to_core())
                for i, (q, e) in enumerate(places)
            ]
            for s, at in [(near, 34), (far, 38)]
        ]

    def send_x(self):
        for copy in self.partner:
            copy.start()

    def pass_x(self, k):
        self.partner[k].wait_recv()

        @pl.when(self.here.has_target)
        def _():
            self.relay[k].start()

        if k == 0:
            self.across[0].start()
        self.share_near[k].start()

    def end_x(self):
        @pl.when(self.here.has_source)
        def _():
            for k in range(3):
                self.relay[k].wait_recv()
                if k == 0:
                    self.across[1].start()
                self.share_far[k].start()

        self.across[0].wait_recv()
        self.share_near[3].start()

        @pl.when(self.here.has_source)
        def _():
            self.across[1].wait_recv()
            self.share_far[3].start()
            for copy in self.share_far:
                copy.wait_recv()

        for copy in self.share_near:
            copy.wait_recv()

    def sum_slots(self, acc, row, prev, last, tiles):
        @pl.loop(0, tiles.shape[0], unroll=UNROLL)
        def _(s):
            product = jnp.dot(self.ext[row[s]], tiles[s], preferred_element_type=jnp.float32)
            acc[s + 1] = acc[prev[s]] + product

        for j, q in enumerate([self.other_core, self.mine_core, self.other, self.mine]):
            for e in range(2):
                k = q * self.owned + e
                self.part[k] = acc[last[k]].astype(jnp.bfloat16)
            if j < 2:
                self.to_core[j].start()

    def sum_chip(self):
        self.to_core[0].wait_recv()
        for e in range(2):
            both = self.part[self.other * self.owned + e].astype(jnp.float32)
            both = both + self.core_in[0, e].astype(jnp.float32)
            self.chip_sum[e] = both.astype(jnp.bfloat16)
            self.to_half[e].start()

    def finish_image(self, diag, dots):
        self.to_core[1].wait_recv()
        blocks = self.part.shape[0]
        for e in range(2):
            self.to_half[e].wait_recv()
            k = self.mine * self.owned + e
            xs = self.ext[blocks + k].astype(jnp.float32)
            both = self.part[k].astype(jnp.float32) + self.core_in[1, e].astype(jnp.float32)
            both = both + self.half_in[e].astype(jnp.float32) + xs * diag[pl.ds(k, 1), :]
            rounded = both.astype(jnp.bfloat16)
            self.own_img[k] = rounded.T
            self.partner_w[e].start()
            self.gather[e].start()
            self.share_own_w[e].start()
            dots[0, pl.ds(k, 1), :] += jnp.sum(xs * rounded.astype(jnp.float32), axis=0, keepdims=True)

    def pass_gathered(self, e):
        self.gather[e].wait_recv()
        self.partner_w[2 + e].start()
        self.share_own_w[2 + e].start()

    def pass_w(self, i):
        self.partner_w[i].wait_recv()

        @pl.when(self.here.has_target)
        def _():
            self.relay_w[i].start()

        self.share_near_w[i].start()

    def end_own_w(self):
        for copy in self.share_own_w:
            copy.wait_recv()
        blocks = self.part.shape[0]

        @pl.loop(0, blocks)
        def _(k):
            self.img[blocks + k] = self.own_img[k]

    def end_w(self):
        @pl.when(self.here.has_source)
        def _():
            for i in range(4):
                self.relay_w[i].wait_recv()
                self.share_far_w[i].start()
            for copy in self.share_far_w:
                copy.wait_recv()

        for copy in self.share_near_w:
            copy.wait_recv()

    def drain(self):
        for copies in [
            self.partner, self.share_near, self.across[:1], self.to_core, self.to_half, self.gather,
            self.partner_w, self.share_own_w, self.share_near_w,
        ]:
            for copy in copies:
                copy.wait_send()

        @pl.when(self.here.has_target)
        def _():
            for copy in self.relay + self.relay_w:
                copy.wait_send()

        @pl.when(self.here.has_source)
        def _():
            for copy in self.share_far + self.across[1:] + self.share_far_w:
                copy.wait_send()


def step_kernel(
    groups, row_hbm, col_hbm, live_hbm, x, tiles_in, diag_in, out, diag_out,
    ext_a, ext_b, img_a, img_b, own_a, own_b, part_a, part_b, core_a, core_b, chip_a, chip_b, half_a, half_b,
    tiles, acc, x_turned, moved, diag_flat, diag, dots, dots_in, row_in, col, live, row, prev, last,
    index_sem, x_sem, tile_sem, diag_sem, send, recv,
):
    here = Place(groups)
    slots = tiles.shape[0]
    samples = x.shape[0]
    blocks = x.shape[1] // B
    cut = samples // HALVES
    scale = STEP / (2.0 * samples)
    a = Half(here, 0, ext_a, img_a, own_a, part_a, core_a, chip_a, half_a, send, recv)
    b = Half(here, COPIES, ext_b, img_b, own_b, part_b, core_b, chip_b, half_b, send, recv)
    dots_core = remote(dots.at[0], dots_in.at[0], send, recv, 2 * COPIES, here.to_core())
    dots_half = remote(dots.at[1], dots_in.at[1], send, recv, 2 * COPIES + 1, here.to_half())

    loads = [
        [
            pltpu.make_async_copy(
                x.at[h * cut : (h + 1) * cut, k * B : (k + 1) * B], half.ext.at[blocks + k], x_sem.at[h, k]
            )
            for k in range(blocks)
        ]
        for h, half in enumerate([a, b])
    ]
    for load in loads[0] + loads[1]:
        load.start()
    index_loads = [
        pltpu.make_async_copy(src, dst, index_sem.at[i])
        for i, (src, dst) in enumerate([(row_hbm, row_in), (col_hbm, col), (live_hbm, live)])
    ]
    for load in index_loads:
        load.start()
    diag_load = pltpu.make_async_copy(diag_in, diag_flat, diag_sem)
    diag_load.start()
    tile_load = pltpu.make_async_copy(tiles_in, tiles, tile_sem)
    tile_load.start()
    here.greet()
    for load in loads[0]:
        load.wait()
    a.send_x()
    for load in index_loads:
        load.wait()

    def latest(column, end):
        def later(t, best):
            return jnp.where(jnp.logical_and(t < live[0], col[t] == column), t + 1, best)

        return lax.fori_loop(0, end, later, jnp.int32(0))

    @pl.loop(0, slots)
    def _(s):
        row[s] = jnp.clip(row_in[s] - (here.g - 1) * blocks, 0, 3 * blocks - 1)
        prev[s] = latest(col[s], s)

    @pl.loop(0, blocks)
    def _(k):
        last[k] = latest(k, slots)

    acc[0] = jnp.zeros_like(acc[0])
    dots[0] = jnp.zeros_like(dots[0])
    diag_load.wait()
    for k in range(blocks):
        diag[k : k + 1, :] = diag_flat[:, k * B : (k + 1) * B]
    for load in loads[1]:
        load.wait()
    tile_load.wait()

    def turn(half, at):
        @pl.loop(0, slots, unroll=UNROLL)
        def _(s):
            x_turned[at, s] = half.ext[row[s]].T

    def own_grad(half, at, s):
        return lax.dot_general(
            x_turned[at, s], half.own_img[col[s]], (((1,), (1,)), ((), ())),
            preferred_element_type=jnp.float32,
        )

    def row_grad(half, s):
        return jnp.dot(half.img[row[s]], half.ext[blocks + col[s]], preferred_element_type=jnp.float32)

    for k in range(3):
        a.pass_x(k)
    b.send_x()
    a.end_x()
    b.pass_x(0)
    a.sum_slots(acc, row, prev, last, tiles)
    b.pass_x(1)
    a.sum_chip()
    b.pass_x(2)
    turn(a, 0)
    b.end_x()
    b.sum_slots(acc, row, prev, last, tiles)
    a.finish_image(diag, dots)
    b.sum_chip()
    for e in range(2):
        a.pass_gathered(e)
        a.pass_w(e)
    turn(b, 1)
    b.finish_image(diag, dots)
    dots_core.start()
    a.pass_w(2)
    a.pass_w(3)
    for e in range(2):
        b.pass_gathered(e)
        b.pass_w(e)
    dots_core.wait_recv()
    dots[1] = dots[0] + dots_in[0]
    dots_half.start()
    a.end_own_w()
    a.end_w()

    def first_half(start, end):
        @pl.loop(start, end, unroll=UNROLL)
        def _(s):
            moved[s] = tiles[s].astype(jnp.float32) - scale * (own_grad(a, 0, s) + row_grad(a, s))

    first_half(0, slots // 2)
    b.pass_w(2)
    first_half(slots // 2, slots)
    b.pass_w(3)
    b.end_own_w()

    @pl.loop(0, slots, unroll=UNROLL)
    def _(s):
        moved[s] -= scale * own_grad(b, 1, s)

    dots_half.wait_recv()
    for k in range(blocks):
        total = dots[1, k : k + 1, :] + dots_in[1, k : k + 1, :]
        old = diag[k : k + 1, :]
        diag_out[:, k * B : (k + 1) * B] = old - STEP * (total / samples - 1.0 / old)
    b.end_w()

    @pl.loop(0, slots, unroll=UNROLL)
    def _(s):
        value = moved[s] - scale * row_grad(b, s)
        kept = jnp.maximum(jnp.abs(value) - STEP * PENALTY, 0.0)
        signed = jnp.where(value < 0, -kept, kept)
        out[s] = jnp.where(s < live[0], signed, 0.0).astype(out.dtype)

    a.drain()
    b.drain()
    dots_core.wait_send()
    dots_half.wait_send()


def step(x, tiles, diag, row, col, live, groups):
    samples, width = x.shape
    slots = tiles.shape[0]
    blocks = width // B
    owned = blocks // 4
    cut = samples // HALVES
    bf16, f32 = jnp.bfloat16, jnp.float32
    vmem = pl.BlockSpec(memory_space=pltpu.VMEM)
    hbm = pl.BlockSpec(memory_space=pl.ANY)

    def twice(*shape):
        return [pltpu.VMEM(shape, bf16)] * 2

    return pl.pallas_call(
        functools.partial(step_kernel, groups),
        out_shape=(
            jax.ShapeDtypeStruct(tiles.shape, bf16),
            jax.ShapeDtypeStruct(diag.shape, f32),
        ),
        in_specs=[hbm] * 6,
        out_specs=(vmem, vmem),
        scratch_shapes=twice(3 * blocks, cut, B)
        + twice(3 * blocks, B, cut)
        + twice(blocks, B, cut)
        + twice(blocks, cut, B)
        + twice(2, owned, cut, B)
        + twice(owned, cut, B)
        + twice(owned, cut, B)
        + [
            pltpu.VMEM(tiles.shape, bf16),
            pltpu.VMEM((slots + 1, cut, B), f32),
            pltpu.VMEM((2, slots, B, cut), bf16),
            pltpu.VMEM((slots, B, B), f32),
            pltpu.VMEM(diag.shape, f32),
            pltpu.VMEM((blocks, B), f32),
            pltpu.VMEM((2, blocks, B), f32),
            pltpu.VMEM((2, blocks, B), f32),
            pltpu.SMEM((slots,), jnp.int32),
            pltpu.SMEM((slots,), jnp.int32),
            pltpu.SMEM((1,), jnp.int32),
            pltpu.SMEM((slots,), jnp.int32),
            pltpu.SMEM((slots,), jnp.int32),
            pltpu.SMEM((blocks,), jnp.int32),
            pltpu.SemaphoreType.DMA((3,)),
            pltpu.SemaphoreType.DMA((2, blocks)),
            pltpu.SemaphoreType.DMA,
            pltpu.SemaphoreType.DMA,
            pltpu.SemaphoreType.DMA((2 * COPIES + 2,)),
            pltpu.SemaphoreType.DMA((2 * COPIES + 2,)),
        ],
        compiler_params=pltpu.CompilerParams(
            collective_id=0, has_side_effects=True, vmem_limit_bytes=VMEM_BYTES
        ),
        name="step",
    )(row, col, live, x, tiles, diag)


def shards(samples, theta_tiles, theta_diag, tile_row, tile_col, tile_count):
    groups = lax.axis_size("blk")
    new_tiles, new_diag = step(
        samples, theta_tiles, theta_diag[None, :], tile_row, tile_col, tile_count, groups
    )
    return (new_tiles, new_diag[0])


def solution(mesh):
    placed = (
        P(None, "blk"),
        P(("blk", "rep"), None, None),
        P("blk"),
        P(("blk", "rep")),
        P(("blk", "rep")),
        P(("blk", "rep")),
    )
    return jax.shard_map(
        shards,
        mesh=mesh,
        in_specs=placed,
        out_specs=(P(("blk", "rep"), None, None), P("blk")),
        check_vma=False,
    )
```

```python
import functools

import jax
import jax.numpy as jnp
from jax import lax
from jax.experimental import pallas as pl
from jax.experimental.pallas import tpu as pltpu
from jax.sharding import PartitionSpec as P

B = 256
STEP = 0.25
PENALTY = 0.5
VMEM_BYTES = 50 * 1024 * 1024


class Place:
    def __init__(self, groups):
        self.g = lax.axis_index("blk")
        self.r = lax.axis_index("rep")
        self.parity = self.g % 2
        self.core = self.r % 2
        self.half = self.r // 2
        self.partner = self.g + 1 - 2 * self.parity
        self.target = self.g + 2 - 4 * self.parity
        self.source = self.g - 2 + 4 * self.parity
        self.has_target = jnp.logical_and(self.target >= 0, self.target < groups)
        self.has_source = jnp.logical_and(self.source >= 0, self.source < groups)
        self.near = 2 * (1 - self.parity)
        self.far = 2 * self.parity

    def to_partner(self):
        return {"blk": self.partner, "rep": self.r}

    def to_target(self):
        return {"blk": self.target, "rep": self.r}

    def to_source(self):
        return {"blk": self.source, "rep": self.r}

    def to_core(self):
        return {"blk": self.g, "rep": self.r + 1 - 2 * self.core}

    def to_half(self):
        return {"blk": self.g, "rep": self.r + 2 - 4 * self.half}

    def greet(self):
        barrier = pltpu.get_barrier_semaphore()

        def signal(device):
            pl.semaphore_signal(
                barrier, inc=1, device_id=device, device_id_type=pl.DeviceIdType.MESH
            )

        signal(self.to_partner())
        signal(self.to_core())
        signal(self.to_half())

        @pl.when(self.has_target)
        def _():
            signal(self.to_target())

        @pl.when(self.has_source)
        def _():
            signal(self.to_source())

        peers = 3 + jnp.where(self.has_target, 1, 0) + jnp.where(self.has_source, 1, 0)
        pl.semaphore_wait(barrier, peers)


def remote(src, dst, send, recv, at, device):
    return pltpu.make_async_remote_copy(
        src_ref=src,
        dst_ref=dst,
        send_sem=send.at[at],
        recv_sem=recv.at[at],
        device_id=device,
        device_id_type=pl.DeviceIdType.MESH,
    )


PARTS = 4
UNROLL = 4
COPIES = 42


class Part:
    def __init__(self, here, first, ext, img, own_img, part, core_in, chip_sum, half_in, send, recv):
        self.here = here
        self.ext, self.img, self.own_img = ext, img, own_img
        self.part, self.core_in, self.chip_sum, self.half_in = part, core_in, chip_sum, half_in
        blocks, samples, _ = part.shape
        unit = samples // 8
        near, far = here.near, here.far
        self.mine = 2 * here.half + here.core
        self.other = 2 * (1 - here.half) + here.core
        self.mine_core = 2 * here.half + 1 - here.core
        self.other_core = 2 * (1 - here.half) + 1 - here.core
        self.owned = blocks // 4
        owned = self.owned

        def copy(src, dst, at, device):
            return remote(src, dst, send, recv, first + at, device)

        shared = 6 * here.half + here.core
        theirs = 6 * (1 - here.half) + here.core
        chunks = [shared, 2 + 2 * here.core, 3 + 2 * here.core]

        def x_at(section, chunk):
            rows = pl.ds(pl.multiple_of(chunk * unit, unit), unit)
            return ext.at[pl.ds(section * blocks, blocks), rows, :]

        self.partner = [
            copy(x_at(1, c), x_at(far, c), k, here.to_partner()) for k, c in enumerate(chunks)
        ]
        self.relay = [
            copy(x_at(near, c), x_at(far, c), 3 + k, here.to_target()) for k, c in enumerate(chunks)
        ]
        self.across = [
            copy(x_at(s, shared), x_at(s, shared), 6 + k, here.to_half()) for k, s in enumerate([near, far])
        ]
        self.share_near, self.share_far = [
            [copy(x_at(s, c), x_at(s, c), at + k, here.to_core()) for k, c in enumerate(chunks + [theirs])]
            for s, at in [(near, 8), (far, 12)]
        ]

        def img_at(section, q, e):
            return img.at[section * blocks + q * owned + e]

        def own_at(q, e):
            return own_img.at[q * owned + e]

        self.to_core = [
            copy(part.at[pl.ds(q * owned, owned)], core_in.at[j], 16 + j, here.to_core())
            for j, q in enumerate([self.other_core, self.mine_core])
        ]
        self.to_half = [copy(chip_sum.at[e], half_in.at[e], 18 + e, here.to_half()) for e in range(2)]
        self.gather = [
            copy(own_at(self.mine, e), own_at(self.mine, e), 20 + e, here.to_half()) for e in range(2)
        ]
        places = [(self.mine, 0), (self.mine, 1), (self.other, 0), (self.other, 1)]
        self.partner_w = [
            copy(own_at(q, e), img_at(far, q, e), 22 + i, here.to_partner())
            for i, (q, e) in enumerate(places)
        ]
        self.relay_w = [
            copy(img_at(near, q, e), img_at(far, q, e), 26 + i, here.to_target())
            for i, (q, e) in enumerate(places)
        ]
        self.share_own_w = [
            copy(own_at(q, e), own_at(q, e), 30 + i, here.to_core()) for i, (q, e) in enumerate(places)
        ]
        self.share_near_w, self.share_far_w = [
            [
                copy(img_at(s, q, e), img_at(s, q, e), at + i, here.to_core())
                for i, (q, e) in enumerate(places)
            ]
            for s, at in [(near, 34), (far, 38)]
        ]

    def send_x(self):
        for copy in self.partner:
            copy.start()

    def pass_x(self, k):
        self.partner[k].wait_recv()

        @pl.when(self.here.has_target)
        def _():
            self.relay[k].start()

        if k == 0:
            self.across[0].start()
        self.share_near[k].start()

    def end_x(self):
        @pl.when(self.here.has_source)
        def _():
            for k in range(3):
                self.relay[k].wait_recv()
                if k == 0:
                    self.across[1].start()
                self.share_far[k].start()

        self.across[0].wait_recv()
        self.share_near[3].start()

        @pl.when(self.here.has_source)
        def _():
            self.across[1].wait_recv()
            self.share_far[3].start()
            for copy in self.share_far:
                copy.wait_recv()

        for copy in self.share_near:
            copy.wait_recv()

    def sum_slots(self, acc, row, prev, last, tiles):
        @pl.loop(0, tiles.shape[0], unroll=UNROLL)
        def _(s):
            product = jnp.dot(self.ext[row[s]], tiles[s], preferred_element_type=jnp.float32)
            acc[s + 1] = acc[prev[s]] + product

        for j, q in enumerate([self.other_core, self.mine_core, self.other, self.mine]):
            for e in range(2):
                k = q * self.owned + e
                self.part[k] = acc[last[k]].astype(jnp.bfloat16)
            if j < 2:
                self.to_core[j].start()

    def sum_chip(self):
        self.to_core[0].wait_recv()
        for e in range(2):
            both = self.part[self.other * self.owned + e].astype(jnp.float32)
            both = both + self.core_in[0, e].astype(jnp.float32)
            self.chip_sum[e] = both.astype(jnp.bfloat16)
            self.to_half[e].start()

    def finish_image(self, diag, dots):
        self.to_core[1].wait_recv()
        blocks = self.part.shape[0]
        for e in range(2):
            self.to_half[e].wait_recv()
            k = self.mine * self.owned + e
            xs = self.ext[blocks + k].astype(jnp.float32)
            both = self.part[k].astype(jnp.float32) + self.core_in[1, e].astype(jnp.float32)
            both = both + self.half_in[e].astype(jnp.float32) + xs * diag[pl.ds(k, 1), :]
            rounded = both.astype(jnp.bfloat16)
            self.own_img[k] = rounded.T
            self.partner_w[e].start()
            self.gather[e].start()
            self.share_own_w[e].start()
            dots[0, pl.ds(k, 1), :] += jnp.sum(xs * rounded.astype(jnp.float32), axis=0, keepdims=True)

    def pass_gathered(self, e):
        self.gather[e].wait_recv()
        self.partner_w[2 + e].start()
        self.share_own_w[2 + e].start()

    def pass_w(self, i):
        self.partner_w[i].wait_recv()

        @pl.when(self.here.has_target)
        def _():
            self.relay_w[i].start()

        self.share_near_w[i].start()

    def end_own_w(self):
        for copy in self.share_own_w:
            copy.wait_recv()
        blocks = self.part.shape[0]

        @pl.loop(0, blocks)
        def _(k):
            self.img[blocks + k] = self.own_img[k]

    def end_w(self):
        @pl.when(self.here.has_source)
        def _():
            for i in range(4):
                self.relay_w[i].wait_recv()
                self.share_far_w[i].start()
            for copy in self.share_far_w:
                copy.wait_recv()

        for copy in self.share_near_w:
            copy.wait_recv()

    def drain(self):
        for copies in [
            self.partner, self.share_near, self.across[:1], self.to_core, self.to_half, self.gather,
            self.partner_w, self.share_own_w, self.share_near_w,
        ]:
            for copy in copies:
                copy.wait_send()

        @pl.when(self.here.has_target)
        def _():
            for copy in self.relay + self.relay_w:
                copy.wait_send()

        @pl.when(self.here.has_source)
        def _():
            for copy in self.share_far + self.across[1:] + self.share_far_w:
                copy.wait_send()


def step_kernel(groups, row_hbm, col_hbm, live_hbm, x, tiles_in, diag_in, out, diag_out, *scratch):
    own_refs, shared_refs = scratch[: 7 * PARTS], scratch[7 * PARTS :]
    (
        tiles, acc, x_turned, moved, diag_flat, diag, dots, dots_in, row_in, col, live, row, prev, last,
        index_sem, x_sem, tile_sem, diag_sem, send, recv,
    ) = shared_refs
    here = Place(groups)
    slots = tiles.shape[0]
    samples = x.shape[0]
    blocks = x.shape[1] // B
    cut = samples // PARTS
    scale = STEP / (2.0 * samples)
    parts = [
        Part(here, p * COPIES, *[own_refs[i * PARTS + p] for i in range(7)], send, recv) for p in range(PARTS)
    ]
    dots_core = remote(dots.at[0], dots_in.at[0], send, recv, PARTS * COPIES, here.to_core())
    dots_half = remote(dots.at[1], dots_in.at[1], send, recv, PARTS * COPIES + 1, here.to_half())

    loads = [
        [
            pltpu.make_async_copy(
                x.at[p * cut : (p + 1) * cut, k * B : (k + 1) * B], part.ext.at[blocks + k], x_sem.at[p, k]
            )
            for k in range(blocks)
        ]
        for p, part in enumerate(parts)
    ]
    for part_loads in loads:
        for load in part_loads:
            load.start()
    index_loads = [
        pltpu.make_async_copy(src, dst, index_sem.at[i])
        for i, (src, dst) in enumerate([(row_hbm, row_in), (col_hbm, col), (live_hbm, live)])
    ]
    for load in index_loads:
        load.start()
    diag_load = pltpu.make_async_copy(diag_in, diag_flat, diag_sem)
    diag_load.start()
    tile_load = pltpu.make_async_copy(tiles_in, tiles, tile_sem)
    tile_load.start()
    here.greet()
    for load in loads[0]:
        load.wait()
    parts[0].send_x()
    for load in index_loads:
        load.wait()

    def latest(column, end):
        def later(t, best):
            return jnp.where(jnp.logical_and(t < live[0], col[t] == column), t + 1, best)

        return lax.fori_loop(0, end, later, jnp.int32(0))

    @pl.loop(0, slots)
    def _(s):
        row[s] = jnp.clip(row_in[s] - (here.g - 1) * blocks, 0, 3 * blocks - 1)
        prev[s] = latest(col[s], s)

    @pl.loop(0, blocks)
    def _(k):
        last[k] = latest(k, slots)

    acc[0] = jnp.zeros_like(acc[0])
    dots[0] = jnp.zeros_like(dots[0])
    diag_load.wait()
    for k in range(blocks):
        diag[k : k + 1, :] = diag_flat[:, k * B : (k + 1) * B]
    for part_loads in loads[1:]:
        for load in part_loads:
            load.wait()
    tile_load.wait()

    def turn(pair):
        @pl.loop(0, slots, unroll=UNROLL)
        def _(s):
            both = [parts[2 * pair + i].ext[row[s]] for i in range(2)]
            x_turned[pair, s] = jnp.concatenate(both, axis=0).T

    def own_grad(pair, s):
        image = [parts[2 * pair + i].own_img[col[s]] for i in range(2)]
        return lax.dot_general(
            x_turned[pair, s], jnp.concatenate(image, axis=1), (((1,), (1,)), ((), ())),
            preferred_element_type=jnp.float32,
        )

    def row_grad(pair, s):
        image = [parts[2 * pair + i].img[row[s]] for i in range(2)]
        data = [parts[2 * pair + i].ext[blocks + col[s]] for i in range(2)]
        return jnp.dot(
            jnp.concatenate(image, axis=1), jnp.concatenate(data, axis=0),
            preferred_element_type=jnp.float32,
        )

    def pass_first(part):
        for e in range(2):
            part.pass_gathered(e)
            part.pass_w(e)

    def pass_second(part):
        part.pass_w(2)
        part.pass_w(3)

    for t in range(PARTS):
        parts[t].pass_x(0)
        if t + 1 < PARTS:
            parts[t + 1].send_x()
        parts[t].pass_x(1)
        parts[t].pass_x(2)
        if t >= 1:
            parts[t - 1].sum_chip()
        if t >= 2:
            parts[t - 2].finish_image(diag, dots)
        if t >= 3:
            pass_first(parts[t - 3])
        parts[t].end_x()
        parts[t].sum_slots(acc, row, prev, last, tiles)
    p0, p1, p2, p3 = parts
    p3.sum_chip()
    p2.finish_image(diag, dots)
    pass_first(p1)
    pass_second(p0)
    turn(0)
    p3.finish_image(diag, dots)
    dots_core.start()
    pass_first(p2)
    pass_second(p1)
    p0.end_own_w()
    p0.end_w()
    pass_first(p3)
    pass_second(p2)
    dots_core.wait_recv()
    dots[1] = dots[0] + dots_in[0]
    dots_half.start()
    turn(1)
    p1.end_own_w()
    p1.end_w()

    def first_pair(start, end):
        @pl.loop(start, end, unroll=UNROLL)
        def _(s):
            moved[s] = tiles[s].astype(jnp.float32) - scale * (own_grad(0, s) + row_grad(0, s))

    first_pair(0, slots // 2)
    p3.pass_w(2)
    first_pair(slots // 2, slots)
    p3.pass_w(3)
    p2.end_own_w()
    p3.end_own_w()

    @pl.loop(0, slots, unroll=UNROLL)
    def _(s):
        moved[s] -= scale * own_grad(1, s)

    dots_half.wait_recv()
    for k in range(blocks):
        total = dots[1, k : k + 1, :] + dots_in[1, k : k + 1, :]
        old = diag[k : k + 1, :]
        diag_out[:, k * B : (k + 1) * B] = old - STEP * (total / samples - 1.0 / old)
    p2.end_w()
    p3.end_w()

    @pl.loop(0, slots, unroll=UNROLL)
    def _(s):
        value = moved[s] - scale * row_grad(1, s)
        kept = jnp.maximum(jnp.abs(value) - STEP * PENALTY, 0.0)
        signed = jnp.where(value < 0, -kept, kept)
        out[s] = jnp.where(s < live[0], signed, 0.0).astype(out.dtype)

    for part in parts:
        part.drain()
    dots_core.wait_send()
    dots_half.wait_send()


def step(x, tiles, diag, row, col, live, groups):
    samples, width = x.shape
    slots = tiles.shape[0]
    blocks = width // B
    owned = blocks // 4
    cut = samples // PARTS
    bf16, f32 = jnp.bfloat16, jnp.float32
    vmem = pl.BlockSpec(memory_space=pltpu.VMEM)
    hbm = pl.BlockSpec(memory_space=pl.ANY)

    def each(*shape):
        return [pltpu.VMEM(shape, bf16)] * PARTS

    return pl.pallas_call(
        functools.partial(step_kernel, groups),
        out_shape=(
            jax.ShapeDtypeStruct(tiles.shape, bf16),
            jax.ShapeDtypeStruct(diag.shape, f32),
        ),
        in_specs=[hbm] * 6,
        out_specs=(vmem, vmem),
        scratch_shapes=each(3 * blocks, cut, B)
        + each(3 * blocks, B, cut)
        + each(blocks, B, cut)
        + each(blocks, cut, B)
        + each(2, owned, cut, B)
        + each(owned, cut, B)
        + each(owned, cut, B)
        + [
            pltpu.VMEM(tiles.shape, bf16),
            pltpu.VMEM((slots + 1, cut, B), f32),
            pltpu.VMEM((PARTS // 2, slots, B, 2 * cut), bf16),
            pltpu.VMEM((slots, B, B), f32),
            pltpu.VMEM(diag.shape, f32),
            pltpu.VMEM((blocks, B), f32),
            pltpu.VMEM((2, blocks, B), f32),
            pltpu.VMEM((2, blocks, B), f32),
            pltpu.SMEM((slots,), jnp.int32),
            pltpu.SMEM((slots,), jnp.int32),
            pltpu.SMEM((1,), jnp.int32),
            pltpu.SMEM((slots,), jnp.int32),
            pltpu.SMEM((slots,), jnp.int32),
            pltpu.SMEM((blocks,), jnp.int32),
            pltpu.SemaphoreType.DMA((3,)),
            pltpu.SemaphoreType.DMA((PARTS, blocks)),
            pltpu.SemaphoreType.DMA,
            pltpu.SemaphoreType.DMA,
            pltpu.SemaphoreType.DMA((PARTS * COPIES + 2,)),
            pltpu.SemaphoreType.DMA((PARTS * COPIES + 2,)),
        ],
        compiler_params=pltpu.CompilerParams(
            collective_id=0, has_side_effects=True, vmem_limit_bytes=VMEM_BYTES
        ),
        name="step",
    )(row, col, live, x, tiles, diag)


def shards(samples, theta_tiles, theta_diag, tile_row, tile_col, tile_count):
    groups = lax.axis_size("blk")
    new_tiles, new_diag = step(
        samples, theta_tiles, theta_diag[None, :], tile_row, tile_col, tile_count, groups
    )
    return (new_tiles, new_diag[0])


def solution(mesh):
    placed = (
        P(None, "blk"),
        P(("blk", "rep"), None, None),
        P("blk"),
        P(("blk", "rep")),
        P(("blk", "rep")),
        P(("blk", "rep")),
    )
    return jax.shard_map(
        shards,
        mesh=mesh,
        in_specs=placed,
        out_specs=(P(("blk", "rep"), None, None), P("blk")),
        check_vma=False,
    )
```

```python
import functools

import jax
import jax.numpy as jnp
from jax import lax
from jax.experimental import pallas as pl
from jax.experimental.pallas import tpu as pltpu
from jax.sharding import PartitionSpec as P

B = 256
STEP = 0.25
PENALTY = 0.5
VMEM_BYTES = 50 * 1024 * 1024


class Place:
    def __init__(self, groups):
        self.g = lax.axis_index("blk")
        self.r = lax.axis_index("rep")
        self.parity = self.g % 2
        self.core = self.r % 2
        self.half = self.r // 2
        self.partner = self.g + 1 - 2 * self.parity
        self.target = self.g + 2 - 4 * self.parity
        self.source = self.g - 2 + 4 * self.parity
        self.has_target = jnp.logical_and(self.target >= 0, self.target < groups)
        self.has_source = jnp.logical_and(self.source >= 0, self.source < groups)
        self.near = 2 * (1 - self.parity)
        self.far = 2 * self.parity

    def to_partner(self):
        return {"blk": self.partner, "rep": self.r}

    def to_target(self):
        return {"blk": self.target, "rep": self.r}

    def to_source(self):
        return {"blk": self.source, "rep": self.r}

    def to_core(self):
        return {"blk": self.g, "rep": self.r + 1 - 2 * self.core}

    def to_half(self):
        return {"blk": self.g, "rep": self.r + 2 - 4 * self.half}

    def greet(self):
        barrier = pltpu.get_barrier_semaphore()

        def signal(device):
            pl.semaphore_signal(
                barrier, inc=1, device_id=device, device_id_type=pl.DeviceIdType.MESH
            )

        signal(self.to_partner())
        signal(self.to_core())
        signal(self.to_half())

        @pl.when(self.has_target)
        def _():
            signal(self.to_target())

        @pl.when(self.has_source)
        def _():
            signal(self.to_source())

        peers = 3 + jnp.where(self.has_target, 1, 0) + jnp.where(self.has_source, 1, 0)
        pl.semaphore_wait(barrier, peers)


def remote(src, dst, send, recv, at, device):
    return pltpu.make_async_remote_copy(
        src_ref=src,
        dst_ref=dst,
        send_sem=send.at[at],
        recv_sem=recv.at[at],
        device_id=device,
        device_id_type=pl.DeviceIdType.MESH,
    )


HALVES = 2
UNROLL = 4
COPIES = 42


class Half:
    def __init__(self, here, first, ext, img, own_img, part, core_in, chip_sum, half_in, send, recv):
        self.here = here
        self.ext, self.img, self.own_img = ext, img, own_img
        self.part, self.core_in, self.chip_sum, self.half_in = part, core_in, chip_sum, half_in
        blocks, samples, _ = part.shape
        unit = samples // 8
        near, far = here.near, here.far
        self.owned = blocks // 2
        self.first = here.core * self.owned
        self.first_core = (1 - here.core) * self.owned

        def copy(src, dst, at, device):
            return remote(src, dst, send, recv, first + at, device)

        shared = 6 * here.half + here.core
        theirs = 6 * (1 - here.half) + here.core
        chunks = [shared, 2 + 2 * here.core, 3 + 2 * here.core]

        def x_at(section, chunk):
            rows = pl.ds(pl.multiple_of(chunk * unit, unit), unit)
            return ext.at[pl.ds(section * blocks, blocks), rows, :]

        self.partner = [
            copy(x_at(1, c), x_at(far, c), k, here.to_partner()) for k, c in enumerate(chunks)
        ]
        self.relay = [
            copy(x_at(near, c), x_at(far, c), 3 + k, here.to_target()) for k, c in enumerate(chunks)
        ]
        self.across = [
            copy(x_at(s, shared), x_at(s, shared), 6 + k, here.to_half()) for k, s in enumerate([near, far])
        ]
        self.share_near, self.share_far = [
            [copy(x_at(s, c), x_at(s, c), at + k, here.to_core()) for k, c in enumerate(chunks + [theirs])]
            for s, at in [(near, 8), (far, 12)]
        ]

        def img_at(section, e):
            return img.at[section * blocks + self.first + e]

        def own_at(e):
            return own_img.at[self.first + e]

        self.pieces = self.owned // 2
        self.to_core = [
            copy(
                part.at[pl.ds(self.first_core + i * self.pieces, self.pieces)],
                core_in.at[pl.ds(i * self.pieces, self.pieces)],
                16 + i,
                here.to_core(),
            )
            for i in range(2)
        ]
        every = range(self.owned)
        size = self.owned
        self.to_half = [copy(chip_sum.at[e], half_in.at[e], 18 + e, here.to_half()) for e in every]
        self.partner_w = [
            copy(own_at(e), img_at(far, e), 18 + size + e, here.to_partner()) for e in every
        ]
        self.relay_w = [
            copy(img_at(near, e), img_at(far, e), 18 + 2 * size + e, here.to_target()) for e in every
        ]
        self.share_own_w = [
            copy(own_at(e), own_at(e), 18 + 3 * size + e, here.to_core()) for e in every
        ]
        self.share_near_w, self.share_far_w = [
            [copy(img_at(s, e), img_at(s, e), 18 + at * size + e, here.to_core()) for e in every]
            for s, at in [(near, 4), (far, 5)]
        ]

    def send_x(self):
        for copy in self.partner:
            copy.start()

    def pass_x(self, k):
        self.partner[k].wait_recv()

        @pl.when(self.here.has_target)
        def _():
            self.relay[k].start()

        if k == 0:
            self.across[0].start()
        self.share_near[k].start()

    def end_x(self):
        @pl.when(self.here.has_source)
        def _():
            for k in range(3):
                self.relay[k].wait_recv()
                if k == 0:
                    self.across[1].start()
                self.share_far[k].start()

        self.across[0].wait_recv()
        self.share_near[3].start()

        @pl.when(self.here.has_source)
        def _():
            self.across[1].wait_recv()
            self.share_far[3].start()
            for copy in self.share_far:
                copy.wait_recv()

        for copy in self.share_near:
            copy.wait_recv()

    def sum_slots(self, acc, row, prev, last, tiles):
        @pl.loop(0, tiles.shape[0], unroll=UNROLL)
        def _(s):
            product = jnp.dot(self.ext[row[s]], tiles[s], preferred_element_type=jnp.float32)
            acc[s + 1] = acc[prev[s]] + product

        for i in range(2):
            for e in range(self.pieces):
                k = self.first_core + i * self.pieces + e
                self.part[k] = acc[last[k]].astype(jnp.bfloat16)
            self.to_core[i].start()
        for e in range(self.owned):
            k = self.first + e
            self.part[k] = acc[last[k]].astype(jnp.bfloat16)

    def sum_chip(self):
        for e in range(self.owned):
            if e % self.pieces == 0:
                self.to_core[e // self.pieces].wait_recv()
            both = self.part[self.first + e].astype(jnp.float32) + self.core_in[e].astype(jnp.float32)
            self.chip_sum[e] = both.astype(jnp.bfloat16)
            self.to_half[e].start()

    def finish_image(self, e, diag, dots):
        blocks = self.part.shape[0]
        self.to_half[e].wait_recv()
        k = self.first + e
        xs = self.ext[blocks + k].astype(jnp.float32)
        both = self.chip_sum[e].astype(jnp.float32) + self.half_in[e].astype(jnp.float32)
        rounded = (both + xs * diag[pl.ds(k, 1), :]).astype(jnp.bfloat16)
        self.own_img[k] = rounded.T
        self.partner_w[e].start()
        self.share_own_w[e].start()
        dots[0, pl.ds(k, 1), :] += jnp.sum(xs * rounded.astype(jnp.float32), axis=0, keepdims=True)

    def pass_w(self, i):
        self.partner_w[i].wait_recv()

        @pl.when(self.here.has_target)
        def _():
            self.relay_w[i].start()

        self.share_near_w[i].start()

    def end_own_w(self):
        for copy in self.share_own_w:
            copy.wait_recv()
        blocks = self.part.shape[0]

        @pl.loop(0, blocks)
        def _(k):
            self.img[blocks + k] = self.own_img[k]

    def end_w(self):
        @pl.when(self.here.has_source)
        def _():
            for i in range(self.owned):
                self.relay_w[i].wait_recv()
                self.share_far_w[i].start()
            for copy in self.share_far_w:
                copy.wait_recv()

        for copy in self.share_near_w:
            copy.wait_recv()

    def drain(self):
        for copies in [
            self.partner, self.share_near, self.across[:1], self.to_core, self.to_half,
            self.partner_w, self.share_own_w, self.share_near_w,
        ]:
            for copy in copies:
                copy.wait_send()

        @pl.when(self.here.has_target)
        def _():
            for copy in self.relay + self.relay_w:
                copy.wait_send()

        @pl.when(self.here.has_source)
        def _():
            for copy in self.share_far + self.across[1:] + self.share_far_w:
                copy.wait_send()


def step_kernel(
    groups, row_hbm, col_hbm, live_hbm, x, tiles_in, diag_in, out, diag_out,
    ext_a, ext_b, img_a, img_b, own_a, own_b, part_a, part_b, core_a, core_b, chip_a, chip_b, half_a, half_b,
    tiles, acc, x_turned, moved, diag_flat, diag, dots, dots_in, row_in, col, live, row, prev, last,
    index_sem, x_sem, tile_sem, diag_sem, send, recv,
):
    here = Place(groups)
    slots = tiles.shape[0]
    samples = x.shape[0]
    blocks = x.shape[1] // B
    cut = samples // HALVES
    scale = STEP / (2.0 * samples)
    a = Half(here, 0, ext_a, img_a, own_a, part_a, core_a, chip_a, half_a, send, recv)
    b = Half(here, COPIES, ext_b, img_b, own_b, part_b, core_b, chip_b, half_b, send, recv)
    dots_core = remote(dots.at[0], dots_in, send, recv, 2 * COPIES, here.to_core())

    loads = [
        [
            pltpu.make_async_copy(
                x.at[h * cut : (h + 1) * cut, k * B : (k + 1) * B], half.ext.at[blocks + k], x_sem.at[h, k]
            )
            for k in range(blocks)
        ]
        for h, half in enumerate([a, b])
    ]
    for load in loads[0] + loads[1]:
        load.start()
    index_loads = [
        pltpu.make_async_copy(src, dst, index_sem.at[i])
        for i, (src, dst) in enumerate([(row_hbm, row_in), (col_hbm, col), (live_hbm, live)])
    ]
    for load in index_loads:
        load.start()
    diag_load = pltpu.make_async_copy(diag_in, diag_flat, diag_sem)
    diag_load.start()
    tile_load = pltpu.make_async_copy(tiles_in, tiles, tile_sem)
    tile_load.start()
    here.greet()
    for load in loads[0]:
        load.wait()
    a.send_x()
    for load in index_loads:
        load.wait()

    def latest(column, end):
        def later(t, best):
            return jnp.where(jnp.logical_and(t < live[0], col[t] == column), t + 1, best)

        return lax.fori_loop(0, end, later, jnp.int32(0))

    @pl.loop(0, slots)
    def _(s):
        row[s] = jnp.clip(row_in[s] - (here.g - 1) * blocks, 0, 3 * blocks - 1)
        prev[s] = latest(col[s], s)

    @pl.loop(0, blocks)
    def _(k):
        last[k] = latest(k, slots)

    acc[0] = jnp.zeros_like(acc[0])
    dots[0] = jnp.zeros_like(dots[0])
    diag_load.wait()
    for k in range(blocks):
        diag[k : k + 1, :] = diag_flat[:, k * B : (k + 1) * B]
    for load in loads[1]:
        load.wait()
    tile_load.wait()

    def turn(half, at):
        @pl.loop(0, slots, unroll=UNROLL)
        def _(s):
            x_turned[at, s] = half.ext[row[s]].T

    def own_grad(half, at, s):
        return lax.dot_general(
            x_turned[at, s], half.own_img[col[s]], (((1,), (1,)), ((), ())),
            preferred_element_type=jnp.float32,
        )

    def row_grad(half, s):
        return jnp.dot(half.img[row[s]], half.ext[blocks + col[s]], preferred_element_type=jnp.float32)

    for k in range(3):
        a.pass_x(k)
    b.send_x()
    a.end_x()
    b.pass_x(0)
    a.sum_slots(acc, row, prev, last, tiles)
    b.pass_x(1)
    a.sum_chip()
    b.pass_x(2)
    turn(a, 0)
    b.end_x()
    b.sum_slots(acc, row, prev, last, tiles)
    a.finish_image(0, diag, dots)
    a.finish_image(1, diag, dots)
    b.sum_chip()
    a.pass_w(0)
    a.finish_image(2, diag, dots)
    a.pass_w(1)
    a.finish_image(3, diag, dots)
    a.pass_w(2)
    turn(b, 1)
    b.finish_image(0, diag, dots)
    a.pass_w(3)
    a.end_own_w()
    b.finish_image(1, diag, dots)
    b.pass_w(0)
    a.end_w()

    def first_half(start, end):
        @pl.loop(start, end, unroll=UNROLL)
        def _(s):
            moved[s] = tiles[s].astype(jnp.float32) - scale * (own_grad(a, 0, s) + row_grad(a, s))

    step_size = slots // 4
    first_half(0, step_size)
    b.finish_image(2, diag, dots)
    b.pass_w(1)
    first_half(step_size, 2 * step_size)
    b.finish_image(3, diag, dots)
    dots_core.start()
    b.pass_w(2)
    first_half(2 * step_size, slots)
    b.pass_w(3)
    b.end_own_w()

    @pl.loop(0, slots, unroll=UNROLL)
    def _(s):
        moved[s] -= scale * own_grad(b, 1, s)

    dots_core.wait_recv()
    for k in range(blocks):
        total = dots[0, k : k + 1, :] + dots_in[k : k + 1, :]
        old = diag[k : k + 1, :]
        diag_out[:, k * B : (k + 1) * B] = old - STEP * (total / samples - 1.0 / old)
    b.end_w()

    @pl.loop(0, slots, unroll=UNROLL)
    def _(s):
        value = moved[s] - scale * row_grad(b, s)
        kept = jnp.maximum(jnp.abs(value) - STEP * PENALTY, 0.0)
        signed = jnp.where(value < 0, -kept, kept)
        out[s] = jnp.where(s < live[0], signed, 0.0).astype(out.dtype)

    a.drain()
    b.drain()
    dots_core.wait_send()


def step(x, tiles, diag, row, col, live, groups):
    samples, width = x.shape
    slots = tiles.shape[0]
    blocks = width // B
    owned = blocks // 2
    cut = samples // HALVES
    bf16, f32 = jnp.bfloat16, jnp.float32
    vmem = pl.BlockSpec(memory_space=pltpu.VMEM)
    hbm = pl.BlockSpec(memory_space=pl.ANY)

    def twice(*shape):
        return [pltpu.VMEM(shape, bf16)] * 2

    return pl.pallas_call(
        functools.partial(step_kernel, groups),
        out_shape=(
            jax.ShapeDtypeStruct(tiles.shape, bf16),
            jax.ShapeDtypeStruct(diag.shape, f32),
        ),
        in_specs=[hbm] * 6,
        out_specs=(vmem, vmem),
        scratch_shapes=twice(3 * blocks, cut, B)
        + twice(3 * blocks, B, cut)
        + twice(blocks, B, cut)
        + twice(blocks, cut, B)
        + twice(owned, cut, B)
        + twice(owned, cut, B)
        + twice(owned, cut, B)
        + [
            pltpu.VMEM(tiles.shape, bf16),
            pltpu.VMEM((slots + 1, cut, B), f32),
            pltpu.VMEM((2, slots, B, cut), bf16),
            pltpu.VMEM((slots, B, B), f32),
            pltpu.VMEM(diag.shape, f32),
            pltpu.VMEM((blocks, B), f32),
            pltpu.VMEM((1, blocks, B), f32),
            pltpu.VMEM((blocks, B), f32),
            pltpu.SMEM((slots,), jnp.int32),
            pltpu.SMEM((slots,), jnp.int32),
            pltpu.SMEM((1,), jnp.int32),
            pltpu.SMEM((slots,), jnp.int32),
            pltpu.SMEM((slots,), jnp.int32),
            pltpu.SMEM((blocks,), jnp.int32),
            pltpu.SemaphoreType.DMA((3,)),
            pltpu.SemaphoreType.DMA((2, blocks)),
            pltpu.SemaphoreType.DMA,
            pltpu.SemaphoreType.DMA,
            pltpu.SemaphoreType.DMA((2 * COPIES + 2,)),
            pltpu.SemaphoreType.DMA((2 * COPIES + 2,)),
        ],
        compiler_params=pltpu.CompilerParams(
            collective_id=0, has_side_effects=True, vmem_limit_bytes=VMEM_BYTES
        ),
        name="step",
    )(row, col, live, x, tiles, diag)


def shards(samples, theta_tiles, theta_diag, tile_row, tile_col, tile_count):
    groups = lax.axis_size("blk")
    new_tiles, new_diag = step(
        samples, theta_tiles, theta_diag[None, :], tile_row, tile_col, tile_count, groups
    )
    return (new_tiles, new_diag[0])


def solution(mesh):
    placed = (
        P(None, "blk"),
        P(("blk", "rep"), None, None),
        P("blk"),
        P(("blk", "rep")),
        P(("blk", "rep")),
        P(("blk", "rep")),
    )
    return jax.shard_map(
        shards,
        mesh=mesh,
        in_specs=placed,
        out_specs=(P(("blk", "rep"), None, None), P("blk")),
        check_vma=False,
    )
```

```python
import functools

import jax
import jax.numpy as jnp
from jax import lax
from jax.experimental import pallas as pl
from jax.experimental.pallas import tpu as pltpu
from jax.sharding import PartitionSpec as P

B = 256
STEP = 0.25
PENALTY = 0.5
VMEM_BYTES = 50 * 1024 * 1024


class Place:
    def __init__(self, groups):
        self.g = lax.axis_index("blk")
        self.r = lax.axis_index("rep")
        self.parity = self.g % 2
        self.core = self.r % 2
        self.half = self.r // 2
        self.partner = self.g + 1 - 2 * self.parity
        self.target = self.g + 2 - 4 * self.parity
        self.source = self.g - 2 + 4 * self.parity
        self.has_target = jnp.logical_and(self.target >= 0, self.target < groups)
        self.has_source = jnp.logical_and(self.source >= 0, self.source < groups)
        self.near = 2 * (1 - self.parity)
        self.far = 2 * self.parity

    def to_partner(self):
        return {"blk": self.partner, "rep": self.r}

    def to_target(self):
        return {"blk": self.target, "rep": self.r}

    def to_source(self):
        return {"blk": self.source, "rep": self.r}

    def to_core(self):
        return {"blk": self.g, "rep": self.r + 1 - 2 * self.core}

    def to_half(self):
        return {"blk": self.g, "rep": self.r + 2 - 4 * self.half}

    def greet(self):
        barrier = pltpu.get_barrier_semaphore()

        def signal(device):
            pl.semaphore_signal(
                barrier, inc=1, device_id=device, device_id_type=pl.DeviceIdType.MESH
            )

        signal(self.to_partner())
        signal(self.to_core())
        signal(self.to_half())

        @pl.when(self.has_target)
        def _():
            signal(self.to_target())

        @pl.when(self.has_source)
        def _():
            signal(self.to_source())

        peers = 3 + jnp.where(self.has_target, 1, 0) + jnp.where(self.has_source, 1, 0)
        pl.semaphore_wait(barrier, peers)


def remote(src, dst, send, recv, at, device):
    return pltpu.make_async_remote_copy(
        src_ref=src,
        dst_ref=dst,
        send_sem=send.at[at],
        recv_sem=recv.at[at],
        device_id=device,
        device_id_type=pl.DeviceIdType.MESH,
    )


HALVES = 2
UNROLL = 8
COPIES = 42


class Half:
    def __init__(self, here, first, ext, img, own_img, part, core_in, chip_sum, half_in, send, recv):
        self.here = here
        self.ext, self.img, self.own_img = ext, img, own_img
        self.part, self.core_in, self.chip_sum, self.half_in = part, core_in, chip_sum, half_in
        blocks, samples, _ = part.shape
        unit = samples // 8
        near, far = here.near, here.far
        self.mine = 2 * here.half + here.core
        self.other = 2 * (1 - here.half) + here.core
        self.mine_core = 2 * here.half + 1 - here.core
        self.other_core = 2 * (1 - here.half) + 1 - here.core
        self.owned = blocks // 4
        owned = self.owned

        def copy(src, dst, at, device):
            return remote(src, dst, send, recv, first + at, device)

        shared = 6 * here.half + here.core
        theirs = 6 * (1 - here.half) + here.core
        chunks = [shared, 2 + 2 * here.core, 3 + 2 * here.core]

        def x_at(section, chunk):
            rows = pl.ds(pl.multiple_of(chunk * unit, unit), unit)
            return ext.at[pl.ds(section * blocks, blocks), rows, :]

        self.partner = [
            copy(x_at(1, c), x_at(far, c), k, here.to_partner()) for k, c in enumerate(chunks)
        ]
        self.relay = [
            copy(x_at(near, c), x_at(far, c), 3 + k, here.to_target()) for k, c in enumerate(chunks)
        ]
        self.across = [
            copy(x_at(s, shared), x_at(s, shared), 6 + k, here.to_half()) for k, s in enumerate([near, far])
        ]
        self.share_near, self.share_far = [
            [copy(x_at(s, c), x_at(s, c), at + k, here.to_core()) for k, c in enumerate(chunks + [theirs])]
            for s, at in [(near, 8), (far, 12)]
        ]

        def img_at(section, q, e):
            return img.at[section * blocks + q * owned + e]

        def own_at(q, e):
            return own_img.at[q * owned + e]

        self.to_core = [
            copy(part.at[pl.ds(q * owned, owned)], core_in.at[j], 16 + j, here.to_core())
            for j, q in enumerate([self.other_core, self.mine_core])
        ]
        self.to_half = [copy(chip_sum.at[e], half_in.at[e], 18 + e, here.to_half()) for e in range(2)]
        self.gather = [
            copy(own_at(self.mine, e), own_at(self.mine, e), 20 + e, here.to_half()) for e in range(2)
        ]
        places = [(self.mine, 0), (self.mine, 1), (self.other, 0), (self.other, 1)]
        self.partner_w = [
            copy(own_at(q, e), img_at(far, q, e), 22 + i, here.to_partner())
            for i, (q, e) in enumerate(places)
        ]
        self.relay_w = [
            copy(img_at(near, q, e), img_at(far, q, e), 26 + i, here.to_target())
            for i, (q, e) in enumerate(places)
        ]
        self.share_own_w = [
            copy(own_at(q, e), own_at(q, e), 30 + i, here.to_core()) for i, (q, e) in enumerate(places)
        ]
        self.share_near_w, self.share_far_w = [
            [
                copy(img_at(s, q, e), img_at(s, q, e), at + i, here.to_core())
                for i, (q, e) in enumerate(places)
            ]
            for s, at in [(near, 34), (far, 38)]
        ]

    def send_x(self):
        for copy in self.partner:
            copy.start()

    def pass_x(self, k):
        self.partner[k].wait_recv()

        @pl.when(self.here.has_target)
        def _():
            self.relay[k].start()

        if k == 0:
            self.across[0].start()
        self.share_near[k].start()

    def end_x(self):
        @pl.when(self.here.has_source)
        def _():
            for k in range(3):
                self.relay[k].wait_recv()
                if k == 0:
                    self.across[1].start()
                self.share_far[k].start()

        self.across[0].wait_recv()
        self.share_near[3].start()

        @pl.when(self.here.has_source)
        def _():
            self.across[1].wait_recv()
            self.share_far[3].start()
            for copy in self.share_far:
                copy.wait_recv()

        for copy in self.share_near:
            copy.wait_recv()

    def sum_slots(self, acc, row, prev, last, tiles):
        @pl.loop(0, tiles.shape[0], unroll=UNROLL)
        def _(s):
            product = jnp.dot(self.ext[row[s]], tiles[s], preferred_element_type=jnp.float32)
            acc[s + 1] = acc[prev[s]] + product

        for j, q in enumerate([self.other_core, self.mine_core, self.other, self.mine]):
            for e in range(2):
                k = q * self.owned + e
                self.part[k] = acc[last[k]].astype(jnp.bfloat16)
            if j < 2:
                self.to_core[j].start()

    def sum_chip(self):
        self.to_core[0].wait_recv()
        for e in range(2):
            both = self.part[self.other * self.owned + e].astype(jnp.float32)
            both = both + self.core_in[0, e].astype(jnp.float32)
            self.chip_sum[e] = both.astype(jnp.bfloat16)
            self.to_half[e].start()

    def finish_image(self, diag, dots):
        self.to_core[1].wait_recv()
        blocks = self.part.shape[0]
        for e in range(2):
            self.to_half[e].wait_recv()
            k = self.mine * self.owned + e
            xs = self.ext[blocks + k].astype(jnp.float32)
            both = self.part[k].astype(jnp.float32) + self.core_in[1, e].astype(jnp.float32)
            both = both + self.half_in[e].astype(jnp.float32) + xs * diag[pl.ds(k, 1), :]
            rounded = both.astype(jnp.bfloat16)
            self.own_img[k] = rounded.T
            self.partner_w[e].start()
            self.gather[e].start()
            self.share_own_w[e].start()
            dots[0, pl.ds(k, 1), :] += jnp.sum(xs * rounded.astype(jnp.float32), axis=0, keepdims=True)

    def pass_gathered(self, e):
        self.gather[e].wait_recv()
        self.partner_w[2 + e].start()
        self.share_own_w[2 + e].start()

    def pass_w(self, i):
        self.partner_w[i].wait_recv()

        @pl.when(self.here.has_target)
        def _():
            self.relay_w[i].start()

        self.share_near_w[i].start()

    def end_own_w(self):
        for copy in self.share_own_w:
            copy.wait_recv()
        blocks = self.part.shape[0]

        @pl.loop(0, blocks)
        def _(k):
            self.img[blocks + k] = self.own_img[k]

    def end_w(self):
        @pl.when(self.here.has_source)
        def _():
            for i in range(4):
                self.relay_w[i].wait_recv()
                self.share_far_w[i].start()
            for copy in self.share_far_w:
                copy.wait_recv()

        for copy in self.share_near_w:
            copy.wait_recv()

    def drain(self):
        for copies in [
            self.partner, self.share_near, self.across[:1], self.to_core, self.to_half, self.gather,
            self.partner_w, self.share_own_w, self.share_near_w,
        ]:
            for copy in copies:
                copy.wait_send()

        @pl.when(self.here.has_target)
        def _():
            for copy in self.relay + self.relay_w:
                copy.wait_send()

        @pl.when(self.here.has_source)
        def _():
            for copy in self.share_far + self.across[1:] + self.share_far_w:
                copy.wait_send()


def step_kernel(
    groups, row_hbm, col_hbm, live_hbm, x, tiles_in, diag_in, out, diag_out,
    ext_a, ext_b, img_a, img_b, own_a, own_b, part_a, part_b, core_a, core_b, chip_a, chip_b, half_a, half_b,
    tiles, acc, x_turned, moved, diag_flat, diag, dots, dots_in, row_in, col, live, row, prev, last,
    index_sem, x_sem, tile_sem, diag_sem, send, recv,
):
    here = Place(groups)
    slots = tiles.shape[0]
    samples = x.shape[0]
    blocks = x.shape[1] // B
    cut = samples // HALVES
    scale = STEP / (2.0 * samples)
    a = Half(here, 0, ext_a, img_a, own_a, part_a, core_a, chip_a, half_a, send, recv)
    b = Half(here, COPIES, ext_b, img_b, own_b, part_b, core_b, chip_b, half_b, send, recv)
    dots_core = remote(dots.at[0], dots_in.at[0], send, recv, 2 * COPIES, here.to_core())
    dots_half = remote(dots.at[1], dots_in.at[1], send, recv, 2 * COPIES + 1, here.to_half())

    loads = [
        [
            pltpu.make_async_copy(
                x.at[h * cut : (h + 1) * cut, k * B : (k + 1) * B], half.ext.at[blocks + k], x_sem.at[h, k]
            )
            for k in range(blocks)
        ]
        for h, half in enumerate([a, b])
    ]
    for load in loads[0] + loads[1]:
        load.start()
    index_loads = [
        pltpu.make_async_copy(src, dst, index_sem.at[i])
        for i, (src, dst) in enumerate([(row_hbm, row_in), (col_hbm, col), (live_hbm, live)])
    ]
    for load in index_loads:
        load.start()
    diag_load = pltpu.make_async_copy(diag_in, diag_flat, diag_sem)
    diag_load.start()
    tile_load = pltpu.make_async_copy(tiles_in, tiles, tile_sem)
    tile_load.start()
    here.greet()
    for load in loads[0]:
        load.wait()
    a.send_x()
    for load in index_loads:
        load.wait()

    def latest(column, end):
        def later(t, best):
            return jnp.where(jnp.logical_and(t < live[0], col[t] == column), t + 1, best)

        return lax.fori_loop(0, end, later, jnp.int32(0))

    @pl.loop(0, slots)
    def _(s):
        row[s] = jnp.clip(row_in[s] - (here.g - 1) * blocks, 0, 3 * blocks - 1)
        prev[s] = latest(col[s], s)

    @pl.loop(0, blocks)
    def _(k):
        last[k] = latest(k, slots)

    acc[0] = jnp.zeros_like(acc[0])
    dots[0] = jnp.zeros_like(dots[0])
    diag_load.wait()
    for k in range(blocks):
        diag[k : k + 1, :] = diag_flat[:, k * B : (k + 1) * B]
    for load in loads[1]:
        load.wait()
    tile_load.wait()

    def turn(half, at):
        @pl.loop(0, slots, unroll=UNROLL)
        def _(s):
            x_turned[at, s] = half.ext[row[s]].T

    def own_grad(half, at, s):
        return lax.dot_general(
            x_turned[at, s], half.own_img[col[s]], (((1,), (1,)), ((), ())),
            preferred_element_type=jnp.float32,
        )

    def row_grad(half, s):
        return jnp.dot(half.img[row[s]], half.ext[blocks + col[s]], preferred_element_type=jnp.float32)

    for k in range(3):
        a.pass_x(k)
    b.send_x()
    a.end_x()
    b.pass_x(0)
    a.sum_slots(acc, row, prev, last, tiles)
    b.pass_x(1)
    a.sum_chip()
    b.pass_x(2)
    turn(a, 0)
    b.end_x()
    b.sum_slots(acc, row, prev, last, tiles)
    a.finish_image(diag, dots)
    b.sum_chip()
    for e in range(2):
        a.pass_gathered(e)
        a.pass_w(e)
    turn(b, 1)
    b.finish_image(diag, dots)
    dots_core.start()
    a.pass_w(2)
    a.pass_w(3)
    for e in range(2):
        b.pass_gathered(e)
        b.pass_w(e)
    dots_core.wait_recv()
    dots[1] = dots[0] + dots_in[0]
    dots_half.start()
    a.end_own_w()
    a.end_w()

    def first_half(start, end):
        @pl.loop(start, end, unroll=UNROLL)
        def _(s):
            moved[s] = tiles[s].astype(jnp.float32) - scale * (own_grad(a, 0, s) + row_grad(a, s))

    first_half(0, slots // 2)
    b.pass_w(2)
    first_half(slots // 2, slots)
    b.pass_w(3)
    b.end_own_w()

    @pl.loop(0, slots, unroll=UNROLL)
    def _(s):
        moved[s] -= scale * own_grad(b, 1, s)

    dots_half.wait_recv()
    for k in range(blocks):
        total = dots[1, k : k + 1, :] + dots_in[1, k : k + 1, :]
        old = diag[k : k + 1, :]
        diag_out[:, k * B : (k + 1) * B] = old - STEP * (total / samples - 1.0 / old)
    b.end_w()

    @pl.loop(0, slots, unroll=UNROLL)
    def _(s):
        value = moved[s] - scale * row_grad(b, s)
        kept = jnp.maximum(jnp.abs(value) - STEP * PENALTY, 0.0)
        signed = jnp.where(value < 0, -kept, kept)
        out[s] = jnp.where(s < live[0], signed, 0.0).astype(out.dtype)

    a.drain()
    b.drain()
    dots_core.wait_send()
    dots_half.wait_send()


def step(x, tiles, diag, row, col, live, groups):
    samples, width = x.shape
    slots = tiles.shape[0]
    blocks = width // B
    owned = blocks // 4
    cut = samples // HALVES
    bf16, f32 = jnp.bfloat16, jnp.float32
    vmem = pl.BlockSpec(memory_space=pltpu.VMEM)
    hbm = pl.BlockSpec(memory_space=pl.ANY)

    def twice(*shape):
        return [pltpu.VMEM(shape, bf16)] * 2

    return pl.pallas_call(
        functools.partial(step_kernel, groups),
        out_shape=(
            jax.ShapeDtypeStruct(tiles.shape, bf16),
            jax.ShapeDtypeStruct(diag.shape, f32),
        ),
        in_specs=[hbm] * 6,
        out_specs=(vmem, vmem),
        scratch_shapes=twice(3 * blocks, cut, B)
        + twice(3 * blocks, B, cut)
        + twice(blocks, B, cut)
        + twice(blocks, cut, B)
        + twice(2, owned, cut, B)
        + twice(owned, cut, B)
        + twice(owned, cut, B)
        + [
            pltpu.VMEM(tiles.shape, bf16),
            pltpu.VMEM((slots + 1, cut, B), f32),
            pltpu.VMEM((2, slots, B, cut), bf16),
            pltpu.VMEM((slots, B, B), f32),
            pltpu.VMEM(diag.shape, f32),
            pltpu.VMEM((blocks, B), f32),
            pltpu.VMEM((2, blocks, B), f32),
            pltpu.VMEM((2, blocks, B), f32),
            pltpu.SMEM((slots,), jnp.int32),
            pltpu.SMEM((slots,), jnp.int32),
            pltpu.SMEM((1,), jnp.int32),
            pltpu.SMEM((slots,), jnp.int32),
            pltpu.SMEM((slots,), jnp.int32),
            pltpu.SMEM((blocks,), jnp.int32),
            pltpu.SemaphoreType.DMA((3,)),
            pltpu.SemaphoreType.DMA((2, blocks)),
            pltpu.SemaphoreType.DMA,
            pltpu.SemaphoreType.DMA,
            pltpu.SemaphoreType.DMA((2 * COPIES + 2,)),
            pltpu.SemaphoreType.DMA((2 * COPIES + 2,)),
        ],
        compiler_params=pltpu.CompilerParams(
            collective_id=0, has_side_effects=True, vmem_limit_bytes=VMEM_BYTES
        ),
        name="step",
    )(row, col, live, x, tiles, diag)


def shards(samples, theta_tiles, theta_diag, tile_row, tile_col, tile_count):
    groups = lax.axis_size("blk")
    new_tiles, new_diag = step(
        samples, theta_tiles, theta_diag[None, :], tile_row, tile_col, tile_count, groups
    )
    return (new_tiles, new_diag[0])


def solution(mesh):
    placed = (
        P(None, "blk"),
        P(("blk", "rep"), None, None),
        P("blk"),
        P(("blk", "rep")),
        P(("blk", "rep")),
        P(("blk", "rep")),
    )
    return jax.shard_map(
        shards,
        mesh=mesh,
        in_specs=placed,
        out_specs=(P(("blk", "rep"), None, None), P("blk")),
        check_vma=False,
    )
```
